128 devices in a mesh: proj: 8 (over x, core), slab: 16 (over z, y).
Axes of the slice: x: 4, y: 4, z: 4, core: 2. Of those that a mesh axis runs over, the one named last changes fastest.
Arguments:
- projections: bfloat16 [2048, 64, 2048], P(('proj', 'slab')), may hold values from -6 to 6
- intersection: int32 [2048, 2], P(('proj', 'slab')), may hold values from 0 to 15, all different within a row; in each aligned block of 16 rows (0 to 15, 16 to 31, ...) at most 4 rows name the same one
- tiles: int32 [2048, 2], P(('proj', 'slab')), may hold values from 0 to 3
- tile_gain: float32 [4, 2048], replicated, may hold values from 0.25 to 4
- bp_matrix: bfloat16 [4, 2048, 1024], replicated, may hold values from -0.0078125 to 0.0078125
- lift_kernel: float32 [32, 27], replicated, may hold values from -1.25 to 1.25
- lift_bias: float32 [32], replicated, may hold values from -3 to 3
- mix_kernel: bfloat16 [27, 32], replicated, may hold values from -0.21875 to 0.21875
Outputs:
- image: float32 [64, 16, 1024], P('slab', None, 'proj')
The draws below stay inside these ranges and needn't reach their ends.
Inputs may be any that keep to these rules, and one draw needn't show every extreme that they name: `intersection`: each view lists 2 different slabs; among the views of one device no slab is listed more than 4 times, a bound that some block reaches.
All inputs are finite; a program needn't handle non-finite values.
Results may differ from the reference program's by a relative error of at most 0.0047.
Values may be sent and summed in bfloat16 or wider, within the bound.
A program may use at most 128 MiB of HBM per device.

```python
import math
import jax
import jax.numpy as jnp
import numpy as np
from jax import lax

DET = 2048
NY = 16
DROWS = 64
BLK_DEV = 16
TOP = 2
NWT = 4
CH = 32
CAP = 4
VIEWS = 2048
NZ = 64
XW = 1024
N_PROJ = 8
N_SLAB = 16


def set_ends(array, key, least, high):
    longest = array.shape.index(max(array.shape))
    spots = []
    for shift in (0, 1):
        where = [jax.random.randint(jax.random.fold_in(key, axis), (), 0, length) for axis, length in enumerate(array.shape)]
        where[longest] = (where[longest] + shift) % array.shape[longest]
        spots.append(tuple(where))
    return array.at[spots[0]].set(least).at[spots[1]].set(high)


def levels(key, shape, cuts, low, high):
    def one(position, parts):
        heights = jax.random.uniform(jax.random.fold_in(jax.random.fold_in(key, 6), position), (parts,), jnp.float32, low / len(cuts), high / len(cuts))
        return jnp.repeat(jnp.exp(heights), shape[position] // parts).reshape((-1,) + (1,) * (len(shape) - position - 1))

    gain = one(*cuts[0])
    for cut in cuts[1:]:
        gain = gain * one(*cut)
    return gain


def routed_block(key, own, number, rows, count, top, reach, skew):
    ranking = jax.random.permutation(key, count)
    packed, usual = shares(count, rows * top, reach, skew, True), shares(count, rows * top, reach, skew, False)
    places = jnp.arange(count)

    def named(lengths, offset_by):
        used = int((lengths > 0).sum())
        fixed = max(1, used // 4)
        shifted = fixed + (places - fixed + offset_by * (used - fixed)) % max(1, count - fixed)
        return jnp.zeros((count,), jnp.int32).at[ranking[jnp.where(places < fixed, places, shifted)]].set(jnp.asarray(lengths, jnp.int32))

    lengths = jnp.where(number % 4 == 0, named(packed, number // 4), named(usual, number - number // 4 - 1))
    mixed = jax.random.permutation(jax.random.fold_in(own, 3), count)
    giver, receiver = mixed[0:count // 2 * 2:2], mixed[1:count // 2 * 2:2]
    margin = jnp.minimum(lengths[giver] - 1, reach - lengths[receiver]) // 2
    margin = jnp.where((giver == ranking[0]) | (receiver == ranking[0]) | (lengths[receiver] == 0), 0, jnp.maximum(margin, 0))
    shifted = jax.random.randint(jax.random.fold_in(own, 4), (count // 2,), 0, 1 << 20) % (margin + 1)
    lengths = lengths.at[giver].add(-shifted).at[receiver].add(shifted)
    labels = jnp.searchsorted(jnp.cumsum(lengths), jnp.arange(rows * top), side="right").astype(jnp.int32)
    table = labels.reshape(top, rows).T
    table = table[jax.random.permutation(jax.random.fold_in(own, 1), rows)]
    offset_by = jax.random.randint(jax.random.fold_in(own, 2), (rows, 1), 0, top)
    return jnp.take_along_axis(table, (jnp.arange(top)[None, :] + offset_by) % top, axis=1)


def shares(number_of, total, limit, slope, full):
    loads = [(1 << 20) // math.isqrt(standing ** slope) + 1 for standing in range(1, number_of + 1)]
    largest = limit if full else min(limit, max(-(-total // number_of), total * loads[0] // sum(loads)))
    least = 1 if total - largest >= number_of - 1 else 0
    given, surplus = [largest] + [least] * (number_of - 1), total - largest - least * (number_of - 1)
    while surplus > 0:
        candidates = [i for i in range(1, number_of) if given[i] < largest] or [i for i in range(1, number_of) if given[i] < limit]
        pool, left = sum([loads[i] for i in candidates]), surplus
        for i in candidates:
            more = min(limit - given[i], max(1, left * loads[i] // pool), surplus)
            given[i] = given[i] + more
            surplus = surplus - more
    return np.array(given)


def normal_values(rng, extent, spread, most, pieces=(), kind=jnp.bfloat16):
    values = spread * jax.random.normal(rng, extent, jnp.float32)
    if pieces:
        values = values * levels(rng, extent, pieces, -0.22, 0.18)
    return jnp.clip(values, -most, most).astype(kind)


def setup_inputs(seed: int = 0) -> dict:
    key_of = jax.random.split(jax.random.key(seed), 9)
    projections = normal_values(key_of[0], (VIEWS, DROWS, DET), 1.0, 6.0, ((0, 128),))
    intersection_keys = jax.random.split(jax.random.fold_in(key_of[1], 1), VIEWS // BLK_DEV)
    intersection_turns = jax.random.permutation(jax.random.fold_in(key_of[1], 3), VIEWS // BLK_DEV)
    intersection = jax.vmap(lambda own, number: routed_block(jax.random.fold_in(key_of[1], 2), own, number, BLK_DEV, N_SLAB, TOP, CAP, 2))(intersection_keys, intersection_turns).reshape((VIEWS, TOP))
    tiles = set_ends(jax.random.randint(key_of[2], (VIEWS, TOP), 0, NWT), jax.random.fold_in(key_of[2], 1), 0, NWT - 1).astype(jnp.int32)
    tile_gain = jnp.clip(jnp.exp(jax.random.uniform(key_of[3], (NWT, DET), jnp.float32, math.log(0.25), math.log(4.0))), 0.25, 4.0)
    bp_matrix = normal_values(key_of[4], (NWT, DET, XW), (DET * BLK_DEV * N_PROJ * TOP) ** -0.5, 0.0078125)
    lift_kernel = normal_values(key_of[5], (CH, 27), 27 ** -0.5, 1.25, (), jnp.float32)
    lift_bias = normal_values(key_of[6], (CH,), 0.5, 3.0, (), jnp.float32)
    mix_kernel = normal_values(key_of[7], (27, CH), (27 * CH) ** -0.5, 0.21875)
    return dict(projections=projections, intersection=intersection, tiles=tiles, tile_gain=tile_gain, bp_matrix=bp_matrix, lift_kernel=lift_kernel, lift_bias=lift_bias, mix_kernel=mix_kernel)


def hilbert_kernel(size):
    places = jnp.arange(size, dtype=jnp.int32)
    lags = places[None, :] - places[:, None]
    odd = (lags % 2) != 0
    safe = jnp.where(odd, lags, 1).astype(jnp.float32)
    return jnp.where(odd, 2.0 / (math.pi * safe), jnp.float32(0.0)).astype(jnp.bfloat16)


def shifted_stack(padded, depth, height, width):
    planes = []
    for shift_z in range(3):
        for shift_y in range(3):
            for shift_x in range(3):
                planes.append(padded[..., shift_z:shift_z + depth, shift_y:shift_y + height, shift_x:shift_x + width])
    return jnp.stack(planes, 0)


def reference(projections, intersection, tiles, tile_gain, bp_matrix, lift_kernel, lift_bias, mix_kernel):
    kernel = hilbert_kernel(DET)
    filtered = jnp.dot(projections.reshape(VIEWS * DROWS, DET), kernel, preferred_element_type=jnp.float32)
    filtered = filtered.astype(jnp.bfloat16).reshape(VIEWS, DROWS, DET).astype(jnp.float32)
    tile_ids = jnp.arange(NWT, dtype=jnp.int32)
    group_ids = jnp.arange(N_SLAB * NWT, dtype=jnp.int32)
    sums = jnp.zeros((N_SLAB * NWT, DROWS * DET), jnp.float32)
    for which in range(TOP):
        select = (tiles[:, which][:, None] == tile_ids[None, :]).astype(jnp.float32)
        gains = jnp.dot(select, tile_gain, precision=lax.Precision.HIGHEST)
        weighted = (filtered * gains[:, None, :]).astype(jnp.bfloat16).astype(jnp.float32)
        group_of = (intersection[:, which] * NWT + tiles[:, which]).astype(jnp.int32)
        owners = (group_ids[:, None] == group_of[None, :]).astype(jnp.float32)
        sums = sums + jnp.dot(owners, weighted.reshape(VIEWS, DROWS * DET), precision=lax.Precision.HIGHEST)
    sums = sums.reshape(N_SLAB, NWT, DROWS, DET)
    volume = jnp.zeros((N_SLAB * DROWS, XW), jnp.float32)
    for tile in range(NWT):
        block = sums[:, tile].reshape(N_SLAB * DROWS, DET)
        volume = volume + jnp.dot(block, bp_matrix[tile].astype(jnp.float32), precision=lax.Precision.HIGHEST)
    volume = volume.reshape(NZ, NY, XW)
    padded = jnp.pad(volume, 1)
    stack = shifted_stack(padded, NZ, NY, XW)
    lifted = jnp.einsum("co,ozyx->czyx", lift_kernel, stack, precision=lax.Precision.HIGHEST)
    features = jnp.maximum(lifted + lift_bias[:, None, None, None], 0.0).astype(jnp.bfloat16)
    frame = jnp.pad(features, ((0, 0), (1, 1), (1, 1), (1, 1)))
    mixed = jnp.einsum("oc,czyx->ozyx", mix_kernel.astype(jnp.float32), frame.astype(jnp.float32))
    image = volume
    for shift_z in range(3):
        for shift_y in range(3):
            for shift_x in range(3):
                offset = 9 * shift_z + 3 * shift_y + shift_x
                image = image + mixed[offset, shift_z:shift_z + NZ, shift_y:shift_y + NY, shift_x:shift_x + XW]
    return image
```

```python
import functools
import math

import jax
import jax.numpy as jnp
import ml_dtypes
import numpy as np
from jax import lax
from jax.experimental import pallas as pl
from jax.experimental.pallas import tpu as pltpu
from jax.sharding import PartitionSpec as P

VZ = 4
NY = 16
NB = 11
SLOTS = 4 * NB
WID = 256


def lag_strip(det):
    lag = (det - WID) + np.arange(WID)[None, :] - np.arange(2 * det - WID)[:, None]
    odd = lag % 2 != 0
    safe = np.where(odd, lag, 1).astype(np.float32)
    values = np.where(odd, np.float32(2.0) / (np.float32(math.pi) * safe), np.float32(0.0))
    return values.astype(ml_dtypes.bfloat16)


def route(inter, tiles):
    def column(a):
        nv = a.shape[0]
        return jnp.concatenate(
            [jnp.broadcast_to(a[:, k : k + 1], (nv, 128)) for k in range(2)], axis=0
        )

    tb, sb = column(tiles), column(inter)
    n = tb.shape[0]
    row = lax.broadcasted_iota(jnp.int32, (n, 128), 0)
    lane = lax.broadcasted_iota(jnp.int32, (n, 128), 1)
    lane1 = lane[0:1]

    def rank(col):
        across = jnp.sum(jnp.where(row == lane, col, 0), axis=0, keepdims=True)
        same = jnp.where((col == across) & (lane < row), 1, 0)
        return jnp.sum(same, axis=1, keepdims=True)

    ends = []
    total = jnp.zeros((1, 128), jnp.int32)
    for t in range(3):
        count = jnp.sum(jnp.where(tb == t, 1, 0), axis=0, keepdims=True)
        total = total + ((count + 3) >> 2)
        ends.append(total)
    base = jnp.where(tb == 0, 0, jnp.where(tb == 1, ends[0], jnp.where(tb == 2, ends[1], ends[2])))
    slot = 4 * base + rank(tb)
    view_row = jnp.sum(jnp.where(slot == lane, row & 15, 0), axis=0, keepdims=True)
    tile_row = sum(jnp.where(lane1 >= e, 1, 0) for e in ends)
    order = rank(sb)
    picks = [
        jnp.sum(jnp.where((sb == lane) & (order == r), slot - SLOTS, 0), axis=0, keepdims=True) + SLOTS
        for r in range(4)
    ]
    return jnp.concatenate([view_row, tile_row, view_row, tile_row] + picks, axis=0)


def kernel(
    proj_ref, strip_ref, gain_ref, inter_ref, tiles_ref, bp_ref, out_ref,
    pv, ks, bpv, fv, wv, rv, planv, plan, sems,
):
    rows, det = pv.shape
    loads = [
        pltpu.make_async_copy(proj_ref, pv, sems.at[0]),
        pltpu.make_async_copy(strip_ref, ks, sems.at[1]),
        pltpu.make_async_copy(bp_ref, bpv, sems.at[2]),
    ]
    for c in loads:
        c.start()
    planv[...] = route(inter_ref[...], tiles_ref[...])
    to_smem = pltpu.make_async_copy(planv, plan, sems.at[3])
    to_smem.start()
    rv[SLOTS * 64 :, :] = jnp.zeros((64, WID), jnp.float32)
    to_smem.wait()
    loads[0].wait()
    loads[1].wait()

    @pl.loop(0, det // WID)
    def _(b):
        k = ks[pl.ds(pl.multiple_of((det - WID) - b * WID, WID), det), :]
        acc = jnp.dot(pv[...], k, preferred_element_type=jnp.float32)
        fv[:, pl.ds(pl.multiple_of(b * WID, WID), WID)] = acc.astype(jnp.bfloat16)

    @pl.loop(0, SLOTS)
    def _(q):
        v = plan[0, q]
        t = plan[1, q // 4]
        f = fv[pl.ds(pl.multiple_of(v * 64, 64), 64), :].astype(jnp.float32)
        g = gain_ref[pl.ds(t, 1), :]
        wv[pl.ds(pl.multiple_of(q * 64, 64), 64), :] = (f * g).astype(jnp.bfloat16)

    loads[2].wait()

    for j in range(4):
        @pl.loop(0, NB)
        def _(b):
            t = plan[1, b]
            at = pl.multiple_of(b * WID, WID)
            rv[pl.ds(at, WID), :] = jnp.dot(
                wv[pl.ds(at, WID), :],
                bpv[t, :, j * WID : (j + 1) * WID],
                preferred_element_type=jnp.float32,
            )

        @pl.loop(0, 16)
        def _(s):
            total = None
            for r in range(4):
                q = plan[4 + r, s]
                term = rv[pl.ds(pl.multiple_of(q * 64, 64), 64), :]
                total = term if total is None else total + term
            out_ref[2 * j, s] = total[:, :128]
            out_ref[2 * j + 1, s] = total[:, 128:]


def backproject(projections, intersection, tiles, tile_gain, bp_matrix):
    nblk, drows, det = projections.shape
    rows = nblk * drows
    any_spec = pl.BlockSpec(memory_space=pl.ANY)
    vmem = pl.BlockSpec(memory_space=pltpu.VMEM)
    return pl.pallas_call(
        kernel,
        out_shape=jax.ShapeDtypeStruct((8, 16, drows, 128), jnp.float32),
        in_specs=[any_spec, any_spec, vmem, vmem, vmem, any_spec],
        out_specs=vmem,
        scratch_shapes=[
            pltpu.VMEM((rows, det), jnp.bfloat16),
            pltpu.VMEM((2 * det - WID, WID), jnp.bfloat16),
            pltpu.VMEM(bp_matrix.shape, jnp.bfloat16),
            pltpu.VMEM((rows, det), jnp.bfloat16),
            pltpu.VMEM((SLOTS * drows, det), jnp.bfloat16),
            pltpu.VMEM((SLOTS * drows + drows, WID), jnp.float32),
            pltpu.VMEM((8, 128), jnp.int32),
            pltpu.SMEM((8, 128), jnp.int32),
            pltpu.SemaphoreType.DMA((4,)),
        ],
        compiler_params=pltpu.CompilerParams(vmem_limit_bytes=60 * 1024 * 1024),
    )(
        projections.reshape(rows, det), jnp.asarray(lag_strip(det)), tile_gain, intersection, tiles, bp_matrix
    )


def extended(cells, sides, width):
    for axis, dim in sides:
        count = lax.axis_size(axis)
        ends = count - 1
        head = lax.slice_in_dim(cells, 0, width, axis=dim)
        tail = lax.slice_in_dim(cells, cells.shape[dim] - width, cells.shape[dim], axis=dim)
        cells = jnp.concatenate(
            [
                lax.ppermute(tail, axis, [(i, (i + 1) % count) for i in range(ends)]),
                cells,
                lax.ppermute(head, axis, [((i + 1) % count, i) for i in range(ends)]),
            ],
            axis=dim,
        )
    return cells


def shifted_stack(padded, depth, height, width):
    planes = []
    for shift_z in range(3):
        for shift_y in range(3):
            for shift_x in range(3):
                planes.append(
                    padded[
                        ...,
                        shift_z : shift_z + depth,
                        shift_y : shift_y + height,
                        shift_x : shift_x + width,
                    ]
                )
    return jnp.stack(planes, 0)


def shards(
    projections, intersection, tiles, tile_gain, bp_matrix, lift_kernel, lift_bias, mix_kernel
):
    partial = backproject(projections, intersection, tiles, tile_gain, bp_matrix)
    part = lax.psum_scatter(partial, "proj", scatter_dimension=0, tiled=False)
    share = lax.psum_scatter(part, "slab", scatter_dimension=0, tiled=False)
    xcells = share.shape[1]
    volume = share.reshape(VZ, NY, xcells)
    rim = extended(volume, (("proj", 2), ("slab", 0)), 1)
    rim = jnp.pad(rim, ((0, 0), (1, 1), (0, 0)))
    stack = shifted_stack(rim, VZ, NY, xcells)
    lifted = jnp.einsum("co,ozyx->czyx", lift_kernel, stack, precision=lax.Precision.HIGHEST)
    features = jnp.maximum(lifted + lift_bias[:, None, None, None], 0.0).astype(jnp.bfloat16)
    frame = extended(features, (("proj", 3), ("slab", 1)), 1)
    frame = jnp.pad(frame, ((0, 0), (0, 0), (1, 1), (0, 0)))
    mixed = jnp.einsum("oc,czyx->ozyx", mix_kernel, frame, preferred_element_type=jnp.float32)
    image = volume
    for shift_z in range(3):
        for shift_y in range(3):
            for shift_x in range(3):
                offset = 9 * shift_z + 3 * shift_y + shift_x
                image = (
                    image
                    + mixed[
                        offset,
                        shift_z : shift_z + VZ,
                        shift_y : shift_y + NY,
                        shift_x : shift_x + xcells,
                    ]
                )
    return image


def solution(mesh):
    placed = (
        P(("proj", "slab"), None, None),
        P(("proj", "slab"), None),
        P(("proj", "slab"), None),
        P(),
        P(),
        P(),
        P(),
        P(),
    )
    return jax.shard_map(
        shards, mesh=mesh, in_specs=placed, out_specs=P("slab", None, "proj"), check_vma=False
    )
```

```python
import functools
import math

import jax
import jax.numpy as jnp
import ml_dtypes
import numpy as np
from jax import lax
from jax.experimental import pallas as pl
from jax.experimental.pallas import tpu as pltpu
from jax.sharding import PartitionSpec as P

MESH = pl.DeviceIdType.MESH
F32, BF16 = jnp.float32, jnp.bfloat16
VZ = 4
NY = 16
CH = 32
NB = 11
SLOTS = 4 * NB
WID = 256
TURN = (2, 1, 3, 0)


def lag_strip(det):
    lag = (det - WID) + np.arange(WID)[None, :] - np.arange(2 * det - WID)[:, None]
    odd = lag % 2 != 0
    safe = np.where(odd, lag, 1).astype(np.float32)
    values = np.where(odd, np.float32(2.0) / (np.float32(math.pi) * safe), np.float32(0.0))
    return values.astype(ml_dtypes.bfloat16)


def iota(shape, dim):
    return lax.broadcasted_iota(jnp.int32, shape, dim)


def route(inter, tiles):
    nv = inter.shape[1]

    def column(a):
        eye = iota((nv, nv), 0) == iota((nv, nv), 1)
        parts = [
            jnp.sum(jnp.where(eye, a[k : k + 1, :], 0), axis=1, keepdims=True) for k in range(2)
        ]
        return jnp.broadcast_to(jnp.concatenate(parts, axis=0), (2 * nv, 128))

    tb, sb = column(tiles), column(inter)
    row, lane = iota((2 * nv, 128), 0), iota((2 * nv, 128), 1)
    lane1 = lane[0:1]

    def rank(col):
        across = jnp.sum(jnp.where(row == lane, col, 0), axis=0, keepdims=True)
        same = jnp.where((col == across) & (lane < row), 1, 0)
        return jnp.sum(same, axis=1, keepdims=True)

    ends = []
    total = jnp.zeros((1, 128), jnp.int32)
    for t in range(3):
        count = jnp.sum(jnp.where(tb == t, 1, 0), axis=0, keepdims=True)
        total = total + ((count + 3) >> 2)
        ends.append(total)
    base = jnp.where(tb == 0, 0, jnp.where(tb == 1, ends[0], jnp.where(tb == 2, ends[1], ends[2])))
    slot = 4 * base + rank(tb)
    view_row = jnp.sum(jnp.where(slot == lane, row & (nv - 1), 0), axis=0, keepdims=True)
    tile_row = sum(jnp.where(lane1 >= e, 1, 0) for e in ends)
    order = rank(sb)
    picks = [
        jnp.sum(jnp.where((sb == lane) & (order == r), slot - SLOTS, 0), axis=0, keepdims=True) + SLOTS
        for r in range(4)
    ]
    return jnp.concatenate([view_row, tile_row, view_row, tile_row] + picks, axis=0)


def mm(a, b):
    return jnp.dot(a, b, preferred_element_type=F32)


def hot(mask):
    return jnp.where(mask, 1.0, 0.0).astype(BF16)


def lift_matrix(lift, bias):
    rows, cols = NY * CH, 160
    spread = hot((iota((rows, CH), 0) & (CH - 1)) == iota((rows, CH), 1))
    taps = mm(spread, lift.astype(BF16)).astype(BF16)
    o, m = iota((27, cols), 0), iota((27, cols), 1)
    dx, dz = m // 48, (m // 16) % 3
    step = (iota((rows, cols), 1) & (NY - 1)) - iota((rows, cols), 0) // CH + 1
    out = jnp.zeros((rows, cols), F32)
    for dy in range(3):
        pick = hot((o == 9 * dz + 3 * dy + dx) & (m < 144))
        out = out + jnp.where(step == dy, mm(taps, pick), 0.0)
    eye = iota((CH, CH), 0) == iota((CH, CH), 1)
    left = jnp.sum(jnp.where(eye, bias, 0.0), axis=1, keepdims=True)
    lane = iota((CH, cols), 1)
    table = jnp.zeros((CH, cols), F32)
    for k in range(3):
        head = left.astype(BF16).astype(F32)
        table = table + jnp.where(lane == 144 + k, head, 0.0)
        left = left - head
    return (out + mm(spread, table.astype(BF16))).astype(BF16)


def mix_matrix(mix):
    rows, cols = 144, NY * CH
    spread = hot((iota((CH, cols), 1) & (CH - 1)) == iota((CH, cols), 0))
    taps = mm(mix, spread).astype(BF16)
    m, o = iota((rows, 27), 0), iota((rows, 27), 1)
    dz, dx = m // 48, (m // 16) % 3
    step = iota((rows, cols), 1) // CH - (iota((rows, cols), 0) & (NY - 1)) + 1
    out = jnp.zeros((rows, cols), F32)
    for dy in range(3):
        pick = hot(o == 9 * dz + 3 * dy + dx)
        out = out + jnp.where(step == dy, mm(pick, taps), 0.0)
    return out.astype(BF16)


def kernel(
    proj_ref, strip_ref, gain_ref, inter_ref, tiles_ref, bp_ref, lift_ref, bias_ref, mix_ref, out_ref,
    pv, ks, bp0, bp1, bp2, bp3, fa, fb, gainv, wv, rv, own, psend, prec, xsend, xrec, ysend, yrec, vol, hsend, hrec, wlift, wmix,
    planv, plan, lsem, ps, pr, xs, xr, ys, yr, hs, hr,
):
    rows, det = pv.shape
    bpv = (bp0, bp1, bp2, bp3)
    n_proj, n_slab = lax.axis_size("proj"), lax.axis_size("slab")
    p, s = lax.axis_index("proj"), lax.axis_index("slab")
    x, c = p // 2, p % 2

    def at_p(d):
        return lax.rem(p + d + n_proj, n_proj)

    def at_s(d):
        return lax.rem(s + d + n_slab, n_slab)

    load_p = pltpu.make_async_copy(proj_ref, pv, lsem.at[0])
    load_k = pltpu.make_async_copy(strip_ref, ks, lsem.at[1])

    def load_b(jj):
        cols = pl.ds(pl.multiple_of(lax.rem(x + TURN[jj], 4) * WID, WID), WID)
        return pltpu.make_async_copy(bp_ref.at[:, :, cols], bpv[jj], lsem.at[3 + jj])

    load_k.start()
    load_p.start()

    barrier = pltpu.get_barrier_semaphore()
    greet = [(at_p(d), s) for d in (2, 4, 6)]
    greet += [(at_p(d), at_s(e)) for d in (-1, 1) for e in (-1, 0, 1)]
    greet += [(p, at_s(d)) for d in range(1, 16)]
    for dev in greet:
        pl.semaphore_signal(barrier, inc=1, device_id=dev, device_id_type=MESH)

    planv[...] = route(inter_ref[...], tiles_ref[...])
    to_smem = pltpu.make_async_copy(planv, plan, lsem.at[2])
    to_smem.start()
    rv[SLOTS] = jnp.zeros((64, WID), F32)
    for t in range(4):
        for b in range(det // WID):
            gainv[b, t] = jnp.broadcast_to(gain_ref[t : t + 1, b * WID : (b + 1) * WID], (8, WID))
    wlift[...] = lift_matrix(lift_ref[...], bias_ref[...])
    wmix[...] = mix_matrix(mix_ref[...])
    to_smem.wait()
    load_k.wait()
    load_p.wait()
    for jj in range(4):
        load_b(jj).start()

    def filt(b, dst):
        k = ks[pl.ds(pl.multiple_of((det - WID) - b * WID, WID), det), :]
        dst[...] = mm(pv[...], k).reshape(dst.shape)

    def weigh(b, src):
        cols = pl.ds(pl.multiple_of(b * WID, WID), WID)
        for q in range(SLOTS):
            f = src[plan[0, q]].reshape(8, 8, WID)
            g = gainv[b, plan[1, q // 4]]
            wv[q * 64 : q * 64 + 64, cols] = (f * g[None]).reshape(64, WID).astype(BF16)

    filt(0, fa)

    @pl.loop(0, det // WID // 2 - 1)
    def _(i):
        filt(2 * i + 1, fb)
        weigh(2 * i, fa)
        filt(2 * i + 2, fa)
        weigh(2 * i + 1, fb)

    filt(det // WID - 1, fb)
    weigh(det // WID - 2, fa)
    weigh(det // WID - 1, fb)

    pl.semaphore_wait(barrier, len(greet))

    def dots(jj, lo, hi):
        for b in range(lo, hi):
            out = mm(wv[b * WID : (b + 1) * WID, :], bpv[jj][plan[1, b]])
            rv[4 * b : 4 * b + 4] = out.reshape(4, 64, WID)

    def pair(jj):
        return pltpu.make_async_remote_copy(
            src_ref=psend.at[jj], dst_ref=prec.at[jj], send_sem=ps.at[jj], recv_sem=pr.at[jj],
            device_id=(p + 1 - 2 * c, s), device_id_type=MESH,
        )

    def sums(jj):
        @pl.loop(0, n_slab)
        def _(e):
            at = pl.ds(pl.multiple_of(e * 64, 64), 64)
            total = rv[plan[4, e]] + rv[plan[5, e]] + rv[plan[6, e]] + rv[plan[7, e]]
            low, high = total[:, :128], total[:, 128:]
            own[at, :] = jnp.where(c == 0, low, high)
            psend[jj, at, :] = jnp.where(c == 0, high, low).astype(BF16)

        pair(jj).start()

    def to_chip(jj):
        return pltpu.make_async_remote_copy(
            src_ref=xsend.at[jj], dst_ref=xrec.at[jj], send_sem=xs.at[jj], recv_sem=xr.at[jj],
            device_id=(at_p(2 * TURN[jj]), s), device_id_type=MESH,
        )

    def pass_on(jj):
        pair(jj).wait_recv()
        xsend[jj] = (own[...] + prec[jj].astype(F32)).astype(BF16)
        to_chip(jj).start()

    for jj in range(4):
        load_b(jj).wait()
        dots(jj, 0, 4)
        if jj:
            pass_on(jj - 1)
        dots(jj, 4, NB)
        sums(jj)

    pair(3).wait_recv()
    for jj in range(3):
        to_chip(jj).wait_recv()

    def total_of(e):
        at = pl.ds(pl.multiple_of(e * 64, 64), 64)
        total = own[at, :] + prec[3, at, :].astype(F32)
        for jj in range(3):
            total = total + xrec[jj, at, :].astype(F32)
        return total

    def to_slab(d):
        return pltpu.make_async_remote_copy(
            src_ref=ysend.at[d - 1], dst_ref=yrec.at[d - 1], send_sem=ys.at[d - 1], recv_sem=yr.at[d - 1],
            device_id=(p, at_s(d)), device_id_type=MESH,
        )

    @pl.loop(1, n_slab)
    def _(d):
        ysend[d - 1] = total_of(at_s(d)).astype(BF16)
        to_slab(d).start()

    vol[...] = total_of(s)

    @pl.loop(1, n_slab)
    def _(d):
        to_slab(d).wait_recv()
        vol[...] += yrec[d - 1].astype(F32)

    hsend[...] = vol[...].astype(BF16)
    halos = []
    for dp in (-1, 0, 1):
        for ds in (-1, 0, 1):
            if dp == 0 and ds == 0:
                continue
            src = {-1: (0, 32), 0: (0, 64), 1: (32, 32)}[ds]
            dst = {-1: 96, 0: 32, 1: 0}[ds]
            k = len(halos)
            halos.append(
                pltpu.make_async_remote_copy(
                    src_ref=hsend.at[pl.ds(src[0], src[1]), :],
                    dst_ref=hrec.at[1 - dp, pl.ds(dst, src[1]), :],
                    send_sem=hs.at[k], recv_sem=hr.at[k],
                    device_id=(at_p(dp), at_s(ds)), device_id_type=MESH,
                )
            )
    for h in halos:
        h.start()
    hrec[1, 32:96, :] = hsend[...]
    for h in halos:
        h.wait_recv()

    row, lane = iota((128, 128), 0), iota((128, 128), 1)
    inside = ((row >= 32) | (s > 0)) & ((row < 96) | (s < n_slab - 1))
    left = jnp.where(p > 0, hrec[0].astype(F32), 0.0)
    right = jnp.where(p < n_proj - 1, hrec[2].astype(F32), 0.0)
    mid = jnp.where(inside, hrec[1].astype(F32), 0.0)
    edge = jnp.where(inside, jnp.where(lane < 64, right, left), 0.0)
    cells = jnp.concatenate([mid, edge], axis=1)
    shifted = [pltpu.roll(cells, 1, 1), cells, pltpu.roll(cells, 255, 1)]
    shifted = [a.astype(BF16) for a in shifted]
    ones = jnp.ones((16, WID), BF16)
    flane = iota((NY * CH, WID), 1)
    keep = ((flane != 255) | (p > 0)) & ((flane != 128) | (p < n_proj - 1))
    mixed = []
    for zo in range(VZ + 2):
        window = jnp.concatenate([a[16 * zo : 16 * zo + 48] for a in shifted] + [ones], axis=0)
        live = keep
        if zo == 0:
            live = live & (s > 0)
        if zo == VZ + 1:
            live = live & (s < n_slab - 1)
        features = jnp.where(live, jnp.maximum(mm(wlift[...], window), 0.0), 0.0).astype(BF16)
        mixed.append(mm(wmix[...], features))
    for z in range(VZ):
        taps = []
        for dx in range(3):
            at = 16 * dx
            taps.append(sum(mixed[z + dz][48 * dz + at : 48 * dz + at + 16] for dz in range(3)))
        image = taps[1] + pltpu.roll(taps[0], 1, 1) + pltpu.roll(taps[2], 255, 1)
        out_ref[16 * z : 16 * z + 16, :] = vol[16 * z : 16 * z + 16, :] + image[:, :128]

    for jj in range(4):
        pair(jj).wait_send()
    for jj in range(3):
        to_chip(jj).wait_send()

    @pl.loop(1, n_slab)
    def _(d):
        to_slab(d).wait_send()

    for h in halos:
        h.wait_send()


def shards(
    projections, intersection, tiles, tile_gain, bp_matrix, lift_kernel, lift_bias, mix_kernel
):
    nblk, drows, det = projections.shape
    rows = nblk * drows
    hbm = pl.BlockSpec(memory_space=pl.ANY)
    vmem = pl.BlockSpec(memory_space=pltpu.VMEM)
    dma = pltpu.SemaphoreType.DMA
    image = pl.pallas_call(
        kernel,
        out_shape=jax.ShapeDtypeStruct((drows, 128), F32),
        in_specs=[hbm, hbm, vmem, vmem, vmem, hbm, vmem, vmem, vmem],
        out_specs=vmem,
        scratch_shapes=[
            pltpu.VMEM((rows, det), BF16),
            pltpu.VMEM((2 * det - WID, WID), BF16),
            pltpu.VMEM((4, det, WID), BF16),
            pltpu.VMEM((4, det, WID), BF16),
            pltpu.VMEM((4, det, WID), BF16),
            pltpu.VMEM((4, det, WID), BF16),
            pltpu.VMEM((nblk, drows, WID), F32),
            pltpu.VMEM((nblk, drows, WID), F32),
            pltpu.VMEM((det // WID, 4, 8, WID), F32),
            pltpu.VMEM((SLOTS * drows, det), BF16),
            pltpu.VMEM((SLOTS + 1, drows, WID), F32),
            pltpu.VMEM((rows, 128), F32),
            pltpu.VMEM((4, rows, 128), BF16),
            pltpu.VMEM((4, rows, 128), BF16),
            pltpu.VMEM((3, rows, 128), BF16),
            pltpu.VMEM((3, rows, 128), BF16),
            pltpu.VMEM((15, drows, 128), BF16),
            pltpu.VMEM((15, drows, 128), BF16),
            pltpu.VMEM((drows, 128), F32),
            pltpu.VMEM((drows, 128), BF16),
            pltpu.VMEM((3, 128, 128), BF16),
            pltpu.VMEM((NY * CH, 160), BF16),
            pltpu.VMEM((144, NY * CH), BF16),
            pltpu.VMEM((8, 128), jnp.int32),
            pltpu.SMEM((8, 128), jnp.int32),
            dma((7,)), dma((4,)), dma((4,)), dma((3,)), dma((3,)), dma((15,)), dma((15,)), dma((8,)), dma((8,)),
        ],
        compiler_params=pltpu.CompilerParams(
            vmem_limit_bytes=60 * 1024 * 1024, collective_id=0, has_side_effects=True
        ),
    )(
        projections.reshape(rows, det), jnp.asarray(lag_strip(det)), tile_gain, intersection.T, tiles.T,
        bp_matrix, lift_kernel, lift_bias.reshape(1, -1), mix_kernel,
    )
    return image.reshape(VZ, NY, 128)


def solution(mesh):
    split = ("proj", "slab")
    placed = (P(split, None, None), P(split, None), P(split, None), P(), P(), P(), P(), P())
    return jax.shard_map(
        shards, mesh=mesh, in_specs=placed, out_specs=P("slab", None, "proj"), check_vma=False
    )
```

```python
import functools
import math

import jax
import jax.numpy as jnp
import ml_dtypes
import numpy as np
from jax import lax
from jax.experimental import pallas as pl
from jax.experimental.pallas import tpu as pltpu
from jax.sharding import PartitionSpec as P

MESH = pl.DeviceIdType.MESH
F32, BF16 = jnp.float32, jnp.bfloat16
VZ = 4
NY = 16
CH = 32
NB = 11
SLOTS = 4 * NB
WID = 256
TURN = (2, 1, 3, 0)


def lag_strip(det):
    lag = (det - WID) + np.arange(WID)[None, :] - np.arange(2 * det - WID)[:, None]
    odd = lag % 2 != 0
    safe = np.where(odd, lag, 1).astype(np.float32)
    values = np.where(odd, np.float32(2.0) / (np.float32(math.pi) * safe), np.float32(0.0))
    return values.astype(ml_dtypes.bfloat16)


def iota(shape, dim):
    return lax.broadcasted_iota(jnp.int32, shape, dim)


def route(inter, tiles):
    nv = inter.shape[1]

    def column(a):
        eye = iota((nv, nv), 0) == iota((nv, nv), 1)
        parts = [
            jnp.sum(jnp.where(eye, a[k : k + 1, :], 0), axis=1, keepdims=True) for k in range(2)
        ]
        return jnp.broadcast_to(jnp.concatenate(parts, axis=0), (2 * nv, 128))

    tb, sb = column(tiles), column(inter)
    row, lane = iota((2 * nv, 128), 0), iota((2 * nv, 128), 1)
    lane1 = lane[0:1]

    def rank(col):
        across = jnp.sum(jnp.where(row == lane, col, 0), axis=0, keepdims=True)
        same = jnp.where((col == across) & (lane < row), 1, 0)
        return jnp.sum(same, axis=1, keepdims=True)

    ends = []
    total = jnp.zeros((1, 128), jnp.int32)
    for t in range(3):
        count = jnp.sum(jnp.where(tb == t, 1, 0), axis=0, keepdims=True)
        total = total + ((count + 3) >> 2)
        ends.append(total)
    base = jnp.where(tb == 0, 0, jnp.where(tb == 1, ends[0], jnp.where(tb == 2, ends[1], ends[2])))
    slot = 4 * base + rank(tb)
    view_row = jnp.sum(jnp.where(slot == lane, row & (nv - 1), 0), axis=0, keepdims=True)
    tile_row = sum(jnp.where(lane1 >= e, 1, 0) for e in ends)
    order = rank(sb)
    picks = [
        jnp.sum(jnp.where((sb == lane) & (order == r), slot - SLOTS, 0), axis=0, keepdims=True) + SLOTS
        for r in range(4)
    ]
    return jnp.concatenate([view_row, tile_row, view_row, tile_row] + picks, axis=0)


def mm(a, b):
    return jnp.dot(a, b, preferred_element_type=F32)


def hot(mask):
    return jnp.where(mask, 1.0, 0.0).astype(BF16)


def lift_matrix(lift, bias):
    rows, cols = NY * CH, 448
    spread = hot((iota((rows, CH), 0) & (CH - 1)) == iota((rows, CH), 1))
    head = lift.astype(BF16)
    rest = (lift - head.astype(F32)).astype(BF16)
    taps = mm(spread, head).astype(BF16)
    fine = mm(spread, rest).astype(BF16)
    o, m = iota((27, cols), 0), iota((27, cols), 1)
    part = m // 144
    dx, dz = (m % 144) // 48, (m // 16) % 3
    step = (iota((rows, cols), 1) & (NY - 1)) - iota((rows, cols), 0) // CH + 1
    out = jnp.zeros((rows, cols), F32)
    for dy in range(3):
        tap = o == 9 * dz + 3 * dy + dx
        term = mm(taps, hot(tap & (part < 2))) + mm(fine, hot(tap & (part == 2)))
        out = out + jnp.where(step == dy, term, 0.0)
    eye = iota((CH, CH), 0) == iota((CH, CH), 1)
    left = jnp.sum(jnp.where(eye, bias, 0.0), axis=1, keepdims=True)
    lane = iota((CH, cols), 1)
    table = jnp.zeros((CH, cols), F32)
    for k in range(3):
        head = left.astype(BF16).astype(F32)
        table = table + jnp.where(lane == 432 + k, head, 0.0)
        left = left - head
    return (out + mm(spread, table.astype(BF16))).astype(BF16)


def mix_matrix(mix):
    rows, cols = 144, NY * CH
    spread = hot((iota((CH, cols), 1) & (CH - 1)) == iota((CH, cols), 0))
    taps = mm(mix, spread).astype(BF16)
    m, o = iota((rows, 27), 0), iota((rows, 27), 1)
    dz, dx = m // 48, (m // 16) % 3
    step = iota((rows, cols), 1) // CH - (iota((rows, cols), 0) & (NY - 1)) + 1
    out = jnp.zeros((rows, cols), F32)
    for dy in range(3):
        pick = hot(o == 9 * dz + 3 * dy + dx)
        out = out + jnp.where(step == dy, mm(pick, taps), 0.0)
    return out.astype(BF16)


def kernel(
    proj_ref, strip_ref, gain_ref, inter_ref, tiles_ref, bp_ref, lift_ref, bias_ref, mix_ref, out_ref,
    pv, ks, bp0, bp1, bp2, bp3, fa, fb, gainv, wv, rv, own, psend, prec, xsend, xrec, ysend, yrec, mine, vol, hrec, wlift, wmix,
    planv, plan, lsem, ps, pr, xs, xr, ys, yr, hs, hr,
):
    rows, det = pv.shape
    bpv = (bp0, bp1, bp2, bp3)
    n_proj, n_slab = lax.axis_size("proj"), lax.axis_size("slab")
    p, s = lax.axis_index("proj"), lax.axis_index("slab")
    x, c = p // 2, p % 2

    def at_p(d):
        return lax.rem(p + d + n_proj, n_proj)

    def at_s(d):
        return lax.rem(s + d + n_slab, n_slab)

    quarter = rows // 4

    def load_p(m):
        part = pl.ds(m * quarter, quarter)
        return pltpu.make_async_copy(proj_ref.at[part, :], pv.at[part, :], lsem.at[7 + m])

    near, far = pl.ds(det - WID, det), pl.ds(0, det - WID)
    load_near = pltpu.make_async_copy(strip_ref.at[near, :], ks.at[near, :], lsem.at[0])
    load_far = pltpu.make_async_copy(strip_ref.at[far, :], ks.at[far, :], lsem.at[1])
    load_near.start()
    load_p(0).start()
    load_far.start()
    for m in range(1, 4):
        load_p(m).start()

    def load_b(jj):
        cols = pl.ds(pl.multiple_of(lax.rem(x + TURN[jj], 4) * WID, WID), WID)
        return pltpu.make_async_copy(bp_ref.at[:, :, cols], bpv[jj], lsem.at[3 + jj])


    barrier = pltpu.get_barrier_semaphore()
    greet = [(at_p(d), s) for d in (2, 4, 6)]
    greet += [(at_p(d), at_s(e)) for d in (-1, 1) for e in (-1, 0, 1)]
    greet += [(p, at_s(d)) for d in range(1, 16)]
    for dev in greet:
        pl.semaphore_signal(barrier, inc=1, device_id=dev, device_id_type=MESH)

    planv[...] = route(inter_ref[...], tiles_ref[...])
    to_smem = pltpu.make_async_copy(planv, plan, lsem.at[2])
    to_smem.start()
    rv[SLOTS] = jnp.zeros((64, WID), F32)
    for t in range(4):
        for b in range(det // WID):
            gainv[b, t] = jnp.broadcast_to(gain_ref[t : t + 1, b * WID : (b + 1) * WID], (8, WID))
    wlift[...] = lift_matrix(lift_ref[...], bias_ref[...])
    wmix[...] = mix_matrix(mix_ref[...])
    to_smem.wait()
    load_near.wait()

    def filt(b, dst):
        k = ks[pl.ds(pl.multiple_of((det - WID) - b * WID, WID), det), :]
        dst[...] = mm(pv[...], k).reshape(dst.shape)

    def weigh(b, src):
        cols = pl.ds(pl.multiple_of(b * WID, WID), WID)
        for q in range(SLOTS):
            f = src[plan[0, q]].reshape(8, 8, WID)
            g = gainv[b, plan[1, q // 4]]
            wv[q * 64 : q * 64 + 64, cols] = (f * g[None]).reshape(64, WID).astype(BF16)

    near_block = ks[det - WID :, :]
    for m in range(4):
        load_p(m).wait()
        if m == 3:
            load_far.wait()
            for jj in range(4):
                load_b(jj).start()
        fa[4 * m : 4 * m + 4] = mm(pv[m * quarter : (m + 1) * quarter, :], near_block).reshape(4, 64, WID)

    @pl.loop(0, det // WID // 2 - 1)
    def _(i):
        filt(2 * i + 1, fb)
        weigh(2 * i, fa)
        filt(2 * i + 2, fa)
        weigh(2 * i + 1, fb)

    filt(det // WID - 1, fb)
    weigh(det // WID - 2, fa)
    weigh(det // WID - 1, fb)

    pl.semaphore_wait(barrier, len(greet))

    def dots(jj, lo, hi):
        for b in range(lo, hi):
            out = mm(wv[b * WID : (b + 1) * WID, :], bpv[jj][plan[1, b]])
            rv[4 * b : 4 * b + 4] = out.reshape(4, 64, WID)

    def pair(jj):
        return pltpu.make_async_remote_copy(
            src_ref=psend.at[jj], dst_ref=prec.at[jj], send_sem=ps.at[jj], recv_sem=pr.at[jj],
            device_id=(p + 1 - 2 * c, s), device_id_type=MESH,
        )

    def sums(jj):
        @pl.loop(0, n_slab)
        def _(e):
            at = pl.ds(pl.multiple_of(e * 64, 64), 64)
            total = rv[plan[4, e]] + rv[plan[5, e]] + rv[plan[6, e]] + rv[plan[7, e]]
            low, high = total[:, :128], total[:, 128:]
            own[at, :] = jnp.where(c == 0, low, high)
            psend[jj, at, :] = jnp.where(c == 0, high, low).astype(BF16)

        pair(jj).start()

    def to_slab(jj, d):
        k = jj * (n_slab - 1) + d - 1
        return pltpu.make_async_remote_copy(
            src_ref=ysend.at[k], dst_ref=yrec.at[k], send_sem=ys.at[k], recv_sem=yr.at[k],
            device_id=(p, at_s(d)), device_id_type=MESH,
        )

    def to_chip(jj):
        return pltpu.make_async_remote_copy(
            src_ref=xsend.at[jj], dst_ref=xrec.at[jj], send_sem=xs.at[jj], recv_sem=xr.at[jj],
            device_id=(at_p(2 * TURN[jj]), s), device_id_type=MESH,
        )

    def spread(jj):
        pair(jj).wait_recv()

        def of(e):
            at = pl.ds(pl.multiple_of(e * 64, 64), 64)
            return own[at, :] + prec[jj, at, :].astype(F32)

        @pl.loop(1, n_slab)
        def _(d):
            ysend[jj * (n_slab - 1) + d - 1] = of(at_s(d)).astype(BF16)
            to_slab(jj, d).start()

        mine[jj] = of(s)

    def gather(jj):
        @pl.loop(1, n_slab)
        def _(d):
            to_slab(jj, d).wait_recv()

        total = mine[jj]
        for d in range(n_slab - 1):
            total = total + yrec[jj * (n_slab - 1) + d].astype(F32)
        return total

    def pass_on(jj):
        xsend[jj] = gather(jj)
        to_chip(jj).start()

    for jj in range(4):
        load_b(jj).wait()
        dots(jj, 0, 4)
        if jj:
            spread(jj - 1)
        dots(jj, 4, NB)
        if jj > 1:
            pass_on(jj - 2)
        sums(jj)

    pass_on(2)
    spread(3)
    total = gather(3)
    for jj in range(3):
        to_chip(jj).wait_recv()
        total = total + xrec[jj]
    vol[...] = total

    halos = []
    for dp in (-1, 0, 1):
        for ds in (-1, 0, 1):
            if dp == 0 and ds == 0:
                continue
            src = {-1: (0, 32), 0: (0, 64), 1: (32, 32)}[ds]
            dst = {-1: 96, 0: 32, 1: 0}[ds]
            k = len(halos)
            halos.append(
                pltpu.make_async_remote_copy(
                    src_ref=vol.at[pl.ds(src[0], src[1]), :],
                    dst_ref=hrec.at[1 - dp, pl.ds(dst, src[1]), :],
                    send_sem=hs.at[k], recv_sem=hr.at[k],
                    device_id=(at_p(dp), at_s(ds)), device_id_type=MESH,
                )
            )
    for h in halos:
        h.start()
    hrec[1, 32:96, :] = total
    for h in halos:
        h.wait_recv()

    row, lane = iota((128, 128), 0), iota((128, 128), 1)
    inside = ((row >= 32) | (s > 0)) & ((row < 96) | (s < n_slab - 1))
    left = jnp.where(p > 0, hrec[0], 0.0)
    right = jnp.where(p < n_proj - 1, hrec[2], 0.0)
    mid = jnp.where(inside, hrec[1], 0.0)
    edge = jnp.where(inside, jnp.where(lane < 64, right, left), 0.0)
    cells = jnp.concatenate([mid, edge], axis=1)
    shifted = [pltpu.roll(cells, 1, 1), cells, pltpu.roll(cells, 255, 1)]
    high = [a.astype(BF16) for a in shifted]
    low = [(a - h.astype(F32)).astype(BF16) for a, h in zip(shifted, high)]
    ones = jnp.ones((16, WID), BF16)
    flane = iota((NY * CH, WID), 1)
    keep = ((flane != 255) | (p > 0)) & ((flane != 128) | (p < n_proj - 1))
    mixed = []
    for zo in range(VZ + 2):
        window = jnp.concatenate([a[16 * zo : 16 * zo + 48] for a in high + low + high] + [ones], axis=0)
        live = keep
        if zo == 0:
            live = live & (s > 0)
        if zo == VZ + 1:
            live = live & (s < n_slab - 1)
        features = jnp.where(live, jnp.maximum(mm(wlift[...], window), 0.0), 0.0).astype(BF16)
        mixed.append(mm(wmix[...], features))
    for z in range(VZ):
        taps = []
        for dx in range(3):
            at = 16 * dx
            taps.append(sum(mixed[z + dz][48 * dz + at : 48 * dz + at + 16] for dz in range(3)))
        image = taps[1] + pltpu.roll(taps[0], 1, 1) + pltpu.roll(taps[2], 255, 1)
        out_ref[16 * z : 16 * z + 16, :] = vol[16 * z : 16 * z + 16, :] + image[:, :128]

    for jj in range(4):
        pair(jj).wait_send()
    for jj in range(3):
        to_chip(jj).wait_send()

    for jj in range(4):
        @pl.loop(1, n_slab)
        def _(d):
            to_slab(jj, d).wait_send()

    for h in halos:
        h.wait_send()


def shards(
    projections, intersection, tiles, tile_gain, bp_matrix, lift_kernel, lift_bias, mix_kernel
):
    nblk, drows, det = projections.shape
    rows = nblk * drows
    hbm = pl.BlockSpec(memory_space=pl.ANY)
    vmem = pl.BlockSpec(memory_space=pltpu.VMEM)
    dma = pltpu.SemaphoreType.DMA
    image = pl.pallas_call(
        kernel,
        out_shape=jax.ShapeDtypeStruct((drows, 128), F32),
        in_specs=[hbm, hbm, vmem, vmem, vmem, hbm, vmem, vmem, vmem],
        out_specs=vmem,
        scratch_shapes=[
            pltpu.VMEM((rows, det), BF16),
            pltpu.VMEM((2 * det - WID, WID), BF16),
            pltpu.VMEM((4, det, WID), BF16),
            pltpu.VMEM((4, det, WID), BF16),
            pltpu.VMEM((4, det, WID), BF16),
            pltpu.VMEM((4, det, WID), BF16),
            pltpu.VMEM((nblk, drows, WID), F32),
            pltpu.VMEM((nblk, drows, WID), F32),
            pltpu.VMEM((det // WID, 4, 8, WID), F32),
            pltpu.VMEM((SLOTS * drows, det), BF16),
            pltpu.VMEM((SLOTS + 1, drows, WID), F32),
            pltpu.VMEM((rows, 128), F32),
            pltpu.VMEM((4, rows, 128), BF16),
            pltpu.VMEM((4, rows, 128), BF16),
            pltpu.VMEM((3, drows, 128), F32),
            pltpu.VMEM((3, drows, 128), F32),
            pltpu.VMEM((60, drows, 128), BF16),
            pltpu.VMEM((60, drows, 128), BF16),
            pltpu.VMEM((4, drows, 128), F32),
            pltpu.VMEM((drows, 128), F32),
            pltpu.VMEM((3, 128, 128), F32),
            pltpu.VMEM((NY * CH, 448), BF16),
            pltpu.VMEM((144, NY * CH), BF16),
            pltpu.VMEM((8, 128), jnp.int32),
            pltpu.SMEM((8, 128), jnp.int32),
            dma((11,)), dma((4,)), dma((4,)), dma((3,)), dma((3,)), dma((60,)), dma((60,)), dma((8,)), dma((8,)),
        ],
        compiler_params=pltpu.CompilerParams(
            vmem_limit_bytes=60 * 1024 * 1024, collective_id=0, has_side_effects=True
        ),
    )(
        projections.reshape(rows, det), jnp.asarray(lag_strip(det)), tile_gain, intersection.T, tiles.T,
        bp_matrix, lift_kernel, lift_bias.reshape(1, -1), mix_kernel,
    )
    return image.reshape(VZ, NY, 128)


def solution(mesh):
    split = ("proj", "slab")
    placed = (P(split, None, None), P(split, None), P(split, None), P(), P(), P(), P(), P())
    return jax.shard_map(
        shards, mesh=mesh, in_specs=placed, out_specs=P("slab", None, "proj"), check_vma=False
    )
```

```python
import functools
import math

import jax
import jax.numpy as jnp
import ml_dtypes
import numpy as np
from jax import lax
from jax.experimental import pallas as pl
from jax.experimental.pallas import tpu as pltpu
from jax.sharding import PartitionSpec as P

MESH = pl.DeviceIdType.MESH
F32, BF16 = jnp.float32, jnp.bfloat16
VZ = 4
NY = 16
CH = 32
GRP = 3
NB = 13
SLOTS = GRP * NB
WID = 256
TURN = (2, 1, 3, 0)


def lag_strip(det):
    lag = (det - WID) + np.arange(WID)[None, :] - np.arange(2 * det - WID)[:, None]
    odd = lag % 2 != 0
    safe = np.where(odd, lag, 1).astype(np.float32)
    values = np.where(odd, np.float32(2.0) / (np.float32(math.pi) * safe), np.float32(0.0))
    return values.astype(ml_dtypes.bfloat16)


def iota(shape, dim):
    return lax.broadcasted_iota(jnp.int32, shape, dim)


def route(inter, tiles):
    nv = inter.shape[1]

    def column(a):
        eye = iota((nv, nv), 0) == iota((nv, nv), 1)
        parts = [
            jnp.sum(jnp.where(eye, a[k : k + 1, :], 0), axis=1, keepdims=True) for k in range(2)
        ]
        return jnp.broadcast_to(jnp.concatenate(parts, axis=0), (2 * nv, 128))

    tb, sb = column(tiles), column(inter)
    row, lane = iota((2 * nv, 128), 0), iota((2 * nv, 128), 1)
    lane1 = lane[0:1]

    def rank(col):
        across = jnp.sum(jnp.where(row == lane, col, 0), axis=0, keepdims=True)
        same = jnp.where((col == across) & (lane < row), 1, 0)
        return jnp.sum(same, axis=1, keepdims=True)

    ends = []
    total = jnp.zeros((1, 128), jnp.int32)
    for t in range(3):
        count = jnp.sum(jnp.where(tb == t, 1, 0), axis=0, keepdims=True)
        total = total + (((count + GRP - 1) * 171) >> 9)
        ends.append(total)
    base = jnp.where(tb == 0, 0, jnp.where(tb == 1, ends[0], jnp.where(tb == 2, ends[1], ends[2])))
    slot = GRP * base + rank(tb)
    view_row = jnp.sum(jnp.where(slot == lane, row & (nv - 1), 0), axis=0, keepdims=True)
    tile_row = sum(jnp.where(lane1 >= e, 1, 0) for e in ends)
    order = rank(sb)
    picks = [
        jnp.sum(jnp.where((sb == lane) & (order == r), slot - SLOTS, 0), axis=0, keepdims=True) + SLOTS
        for r in range(4)
    ]
    return jnp.concatenate([view_row, tile_row, view_row, tile_row] + picks, axis=0)


def mm(a, b):
    return jnp.dot(a, b, preferred_element_type=F32)


def hot(mask):
    return jnp.where(mask, 1.0, 0.0).astype(BF16)


def lift_matrix(lift, bias):
    rows, cols = NY * CH, 448
    spread = hot((iota((rows, CH), 0) & (CH - 1)) == iota((rows, CH), 1))
    head = lift.astype(BF16)
    rest = (lift - head.astype(F32)).astype(BF16)
    taps = mm(spread, head).astype(BF16)
    fine = mm(spread, rest).astype(BF16)
    o, m = iota((27, cols), 0), iota((27, cols), 1)
    part = m // 144
    dx, dz = (m % 144) // 48, (m // 16) % 3
    step = (iota((rows, cols), 1) & (NY - 1)) - iota((rows, cols), 0) // CH + 1
    out = jnp.zeros((rows, cols), F32)
    for dy in range(3):
        tap = o == 9 * dz + 3 * dy + dx
        term = mm(taps, hot(tap & (part < 2))) + mm(fine, hot(tap & (part == 2)))
        out = out + jnp.where(step == dy, term, 0.0)
    eye = iota((CH, CH), 0) == iota((CH, CH), 1)
    left = jnp.sum(jnp.where(eye, bias, 0.0), axis=1, keepdims=True)
    lane = iota((CH, cols), 1)
    table = jnp.zeros((CH, cols), F32)
    for k in range(3):
        head = left.astype(BF16).astype(F32)
        table = table + jnp.where(lane == 432 + k, head, 0.0)
        left = left - head
    return (out + mm(spread, table.astype(BF16))).astype(BF16)


def mix_matrix(mix):
    rows, cols = 144, NY * CH
    spread = hot((iota((CH, cols), 1) & (CH - 1)) == iota((CH, cols), 0))
    taps = mm(mix, spread).astype(BF16)
    m, o = iota((rows, 27), 0), iota((rows, 27), 1)
    dz, dx = m // 48, (m // 16) % 3
    step = iota((rows, cols), 1) // CH - (iota((rows, cols), 0) & (NY - 1)) + 1
    out = jnp.zeros((rows, cols), F32)
    for dy in range(3):
        pick = hot(o == 9 * dz + 3 * dy + dx)
        out = out + jnp.where(step == dy, mm(pick, taps), 0.0)
    return out.astype(BF16)


def kernel(
    proj_ref, strip_ref, gain_ref, inter_ref, tiles_ref, bp_ref, lift_ref, bias_ref, mix_ref, out_ref,
    pv, ks, bp0, bp1, bp2, bp3, fa, fb, gainv, wv, rv, own, psend, prec, xsend, xrec, ysend, yrec, bsend, brec, mine, vol, hsend, hrec, wlift, wmix,
    planv, plan, lsem, ps, pr, xs, xr, ys, yr, hs, hr,
):
    rows, det = pv.shape
    bpv = (bp0, bp1, bp2, bp3)
    n_proj, n_slab = lax.axis_size("proj"), lax.axis_size("slab")
    p, s = lax.axis_index("proj"), lax.axis_index("slab")
    x, c = p // 2, p % 2

    def at_p(d):
        return lax.rem(p + d + n_proj, n_proj)

    def at_s(d):
        return lax.rem(s + d + n_slab, n_slab)

    quarter = rows // 4

    def load_p(m):
        part = pl.ds(m * quarter, quarter)
        return pltpu.make_async_copy(proj_ref.at[part, :], pv.at[part, :], lsem.at[7 + m])

    near, far = pl.ds(det - WID, det), pl.ds(0, det - WID)
    load_near = pltpu.make_async_copy(strip_ref.at[near, :], ks.at[near, :], lsem.at[0])
    load_far = pltpu.make_async_copy(strip_ref.at[far, :], ks.at[far, :], lsem.at[1])
    load_near.start()
    load_p(0).start()
    load_far.start()
    for m in range(1, 4):
        load_p(m).start()

    def load_b(jj):
        cols = pl.ds(pl.multiple_of(lax.rem(x + TURN[jj], 4) * WID, WID), WID)
        return pltpu.make_async_copy(bp_ref.at[:, :, cols], bpv[jj], lsem.at[3 + jj])


    barrier = pltpu.get_barrier_semaphore()
    greet = [(at_p(d), s) for d in (2, 4, 6)]
    greet += [(at_p(d), at_s(e)) for d in (-1, 1) for e in (-1, 0, 1)]
    greet += [(p, at_s(d)) for d in range(1, 16)]
    for dev in greet:
        pl.semaphore_signal(barrier, inc=1, device_id=dev, device_id_type=MESH)

    planv[...] = route(inter_ref[...], tiles_ref[...])
    to_smem = pltpu.make_async_copy(planv, plan, lsem.at[2])
    to_smem.start()
    rv[SLOTS] = jnp.zeros((64, WID), F32)
    for t in range(4):
        for b in range(det // WID):
            gainv[b, t] = jnp.broadcast_to(gain_ref[t : t + 1, b * WID : (b + 1) * WID], (8, WID))
    wlift[...] = lift_matrix(lift_ref[...], bias_ref[...])
    wmix[...] = mix_matrix(mix_ref[...])
    to_smem.wait()
    load_near.wait()

    def filt(b, dst):
        k = ks[pl.ds(pl.multiple_of((det - WID) - b * WID, WID), det), :]
        dst[...] = mm(pv[...], k).reshape(dst.shape)

    def weigh(b, src):
        cols = pl.ds(pl.multiple_of(b * WID, WID), WID)
        for q in range(SLOTS):
            f = src[plan[0, q]].reshape(8, 8, WID)
            g = gainv[b, plan[1, q // GRP]]
            wv[q * 64 : q * 64 + 64, cols] = (f * g[None]).reshape(64, WID).astype(BF16)

    near_block = ks[det - WID :, :]
    for m in range(4):
        load_p(m).wait()
        if m == 3:
            load_far.wait()
            for jj in range(4):
                load_b(jj).start()
        fa[4 * m : 4 * m + 4] = mm(pv[m * quarter : (m + 1) * quarter, :], near_block).reshape(4, 64, WID)

    @pl.loop(0, det // WID // 2 - 1)
    def _(i):
        filt(2 * i + 1, fb)
        weigh(2 * i, fa)
        filt(2 * i + 2, fa)
        weigh(2 * i + 1, fb)

    filt(det // WID - 1, fb)
    weigh(det // WID - 2, fa)
    weigh(det // WID - 1, fb)

    pl.semaphore_wait(barrier, len(greet))

    def dots(jj, lo, hi):
        for b in range(lo, hi):
            out = mm(wv[b * GRP * 64 : (b + 1) * GRP * 64, :], bpv[jj][plan[1, b]])
            rv[GRP * b : GRP * b + GRP] = out.reshape(GRP, 64, WID)

    def pair(jj):
        return pltpu.make_async_remote_copy(
            src_ref=psend.at[jj], dst_ref=prec.at[jj], send_sem=ps.at[jj], recv_sem=pr.at[jj],
            device_id=(p + 1 - 2 * c, s), device_id_type=MESH,
        )

    def sums(jj):
        @pl.loop(0, n_slab)
        def _(e):
            at = pl.ds(pl.multiple_of(e * 64, 64), 64)
            total = rv[plan[4, e]] + rv[plan[5, e]] + rv[plan[6, e]] + rv[plan[7, e]]
            low, high = total[:, :128], total[:, 128:]
            own[at, :] = jnp.where(c == 0, low, high)
            psend[jj, at, :] = jnp.where(c == 0, high, low).astype(BF16)

        pair(jj).start()

    def to_slab(k, d):
        k = k * (n_slab - 1) + d - 1
        return pltpu.make_async_remote_copy(
            src_ref=ysend.at[k], dst_ref=yrec.at[k], send_sem=ys.at[k], recv_sem=yr.at[k],
            device_id=(p, at_s(d)), device_id_type=MESH,
        )

    def to_chip(jj):
        src, dst = (bsend, brec) if jj == 0 else (xsend.at[jj - 1], xrec.at[jj - 1])
        return pltpu.make_async_remote_copy(
            src_ref=src, dst_ref=dst, send_sem=xs.at[jj], recv_sem=xr.at[jj],
            device_id=(at_p(2 * TURN[jj]), s), device_id_type=MESH,
        )

    def spread(k, jj):
        pair(jj).wait_recv()
        if jj == 3:
            to_chip(1).wait_recv()
            to_chip(2).wait_recv()

        def of(e):
            at = pl.ds(pl.multiple_of(e * 64, 64), 64)
            total = own[at, :] + prec[jj, at, :].astype(F32)
            if jj == 3:
                total = total + (xrec[0, at, :].astype(F32) + xrec[1, at, :].astype(F32))
            return total

        @pl.loop(1, n_slab, unroll=5)
        def _(d):
            ysend[k * (n_slab - 1) + d - 1] = of(at_s(d)).astype(BF16)
            to_slab(k, d).start()

        mine[k] = of(s)

    def gather(k):
        total = mine[k]
        for d in range(1, n_slab):
            to_slab(k, d).wait_recv()
            total = total + yrec[k * (n_slab - 1) + d - 1].astype(F32)
        return total

    def pass_on(jj):
        pair(jj).wait_recv()
        xsend[jj - 1] = (own[...] + prec[jj].astype(F32)).astype(BF16)
        to_chip(jj).start()

    for jj in range(4):
        load_b(jj).wait()
        dots(jj, 0, 5)
        if jj == 1:
            spread(0, 0)
        elif jj > 1:
            pass_on(jj - 1)
        dots(jj, 5, NB)
        if jj == 2:
            bsend[...] = gather(0)
            to_chip(0).start()
        sums(jj)

    spread(1, 3)
    to_chip(0).wait_recv()
    total = gather(1) + brec[...]
    vol[...] = total
    hsend[...] = total.astype(BF16)

    halos = []
    for dp in (-1, 0, 1):
        for ds in (-1, 0, 1):
            if dp == 0 and ds == 0:
                continue
            src = {-1: (0, 32), 0: (0, 64), 1: (32, 32)}[ds]
            dst = {-1: 96, 0: 32, 1: 0}[ds]
            k = len(halos)
            halos.append(
                pltpu.make_async_remote_copy(
                    src_ref=hsend.at[pl.ds(src[0], src[1]), :],
                    dst_ref=hrec.at[1 - dp, pl.ds(dst, src[1]), :],
                    send_sem=hs.at[k], recv_sem=hr.at[k],
                    device_id=(at_p(dp), at_s(ds)), device_id_type=MESH,
                )
            )
    for h in halos:
        h.start()
    for h in halos:
        h.wait_recv()

    row, lane = iota((128, 128), 0), iota((128, 128), 1)
    inside = ((row >= 32) | (s > 0)) & ((row < 96) | (s < n_slab - 1))
    left = jnp.where(p > 0, hrec[0].astype(F32), 0.0)
    right = jnp.where(p < n_proj - 1, hrec[2].astype(F32), 0.0)
    mid = jnp.concatenate([hrec[1, :32].astype(F32), total, hrec[1, 96:].astype(F32)], axis=0)
    mid = jnp.where(inside, mid, 0.0)
    edge = jnp.where(inside, jnp.where(lane < 64, right, left), 0.0)
    cells = jnp.concatenate([mid, edge], axis=1)
    shifted = [pltpu.roll(cells, 1, 1), cells, pltpu.roll(cells, 255, 1)]
    high = [a.astype(BF16) for a in shifted]
    low = [(a - h.astype(F32)).astype(BF16) for a, h in zip(shifted, high)]
    ones = jnp.ones((16, WID), BF16)
    flane = iota((NY * CH, WID), 1)
    keep = ((flane != 255) | (p > 0)) & ((flane != 128) | (p < n_proj - 1))
    mixed = []
    for zo in range(VZ + 2):
        window = jnp.concatenate([a[16 * zo : 16 * zo + 48] for a in high + low + high] + [ones], axis=0)
        live = keep
        if zo == 0:
            live = live & (s > 0)
        if zo == VZ + 1:
            live = live & (s < n_slab - 1)
        features = jnp.where(live, jnp.maximum(mm(wlift[...], window), 0.0), 0.0).astype(BF16)
        mixed.append(mm(wmix[...], features))
    for z in range(VZ):
        taps = []
        for dx in range(3):
            at = 16 * dx
            taps.append(sum(mixed[z + dz][48 * dz + at : 48 * dz + at + 16] for dz in range(3)))
        image = taps[1] + pltpu.roll(taps[0], 1, 1) + pltpu.roll(taps[2], 255, 1)
        out_ref[16 * z : 16 * z + 16, :] = vol[16 * z : 16 * z + 16, :] + image[:, :128]

    for jj in range(4):
        pair(jj).wait_send()
    for jj in range(3):
        to_chip(jj).wait_send()

    for k in range(2):
        @pl.loop(1, n_slab)
        def _(d):
            to_slab(k, d).wait_send()

    for h in halos:
        h.wait_send()


def shards(
    projections, intersection, tiles, tile_gain, bp_matrix, lift_kernel, lift_bias, mix_kernel
):
    nblk, drows, det = projections.shape
    rows = nblk * drows
    hbm = pl.BlockSpec(memory_space=pl.ANY)
    vmem = pl.BlockSpec(memory_space=pltpu.VMEM)
    dma = pltpu.SemaphoreType.DMA
    image = pl.pallas_call(
        kernel,
        out_shape=jax.ShapeDtypeStruct((drows, 128), F32),
        in_specs=[hbm, hbm, vmem, vmem, vmem, hbm, vmem, vmem, vmem],
        out_specs=vmem,
        scratch_shapes=[
            pltpu.VMEM((rows, det), BF16),
            pltpu.VMEM((2 * det - WID, WID), BF16),
            pltpu.VMEM((4, det, WID), BF16),
            pltpu.VMEM((4, det, WID), BF16),
            pltpu.VMEM((4, det, WID), BF16),
            pltpu.VMEM((4, det, WID), BF16),
            pltpu.VMEM((nblk, drows, WID), F32),
            pltpu.VMEM((nblk, drows, WID), F32),
            pltpu.VMEM((det // WID, 4, 8, WID), F32),
            pltpu.VMEM((SLOTS * drows, det), BF16),
            pltpu.VMEM((SLOTS + 1, drows, WID), F32),
            pltpu.VMEM((rows, 128), F32),
            pltpu.VMEM((4, rows, 128), BF16),
            pltpu.VMEM((4, rows, 128), BF16),
            pltpu.VMEM((2, rows, 128), BF16),
            pltpu.VMEM((2, rows, 128), BF16),
            pltpu.VMEM((30, drows, 128), BF16),
            pltpu.VMEM((30, drows, 128), BF16),
            pltpu.VMEM((drows, 128), F32),
            pltpu.VMEM((drows, 128), F32),
            pltpu.VMEM((2, drows, 128), F32),
            pltpu.VMEM((drows, 128), F32),
            pltpu.VMEM((drows, 128), BF16),
            pltpu.VMEM((3, 128, 128), BF16),
            pltpu.VMEM((NY * CH, 448), BF16),
            pltpu.VMEM((144, NY * CH), BF16),
            pltpu.VMEM((8, 128), jnp.int32),
            pltpu.SMEM((8, 128), jnp.int32),
            dma((11,)), dma((4,)), dma((4,)), dma((3,)), dma((3,)), dma((30,)), dma((30,)), dma((8,)), dma((8,)),
        ],
        compiler_params=pltpu.CompilerParams(
            vmem_limit_bytes=60 * 1024 * 1024, collective_id=0, has_side_effects=True
        ),
    )(
        projections.reshape(rows, det), jnp.asarray(lag_strip(det)), tile_gain, intersection.T, tiles.T,
        bp_matrix, lift_kernel, lift_bias.reshape(1, -1), mix_kernel,
    )
    return image.reshape(VZ, NY, 128)


def solution(mesh):
    split = ("proj", "slab")
    placed = (P(split, None, None), P(split, None), P(split, None), P(), P(), P(), P(), P())
    return jax.shard_map(
        shards, mesh=mesh, in_specs=placed, out_specs=P("slab", None, "proj"), check_vma=False
    )
```

```python
import functools
import math

import jax
import jax.numpy as jnp
import ml_dtypes
import numpy as np
from jax import lax
from jax.experimental import pallas as pl
from jax.experimental.pallas import tpu as pltpu
from jax.sharding import PartitionSpec as P

MESH = pl.DeviceIdType.MESH
F32, BF16 = jnp.float32, jnp.bfloat16
VZ = 4
NY = 16
CH = 32
GRP = 3
NB = 13
SLOTS = GRP * NB
WID = 256
TURN = (2, 1, 3, 0)


def lag_strip(det):
    lag = (det - WID) + np.arange(WID)[None, :] - np.arange(2 * det - WID)[:, None]
    odd = lag % 2 != 0
    safe = np.where(odd, lag, 1).astype(np.float32)
    values = np.where(odd, np.float32(2.0) / (np.float32(math.pi) * safe), np.float32(0.0))
    return values.astype(ml_dtypes.bfloat16)


def iota(shape, dim):
    return lax.broadcasted_iota(jnp.int32, shape, dim)


def route(inter, tiles):
    nv = inter.shape[1]

    def column(a):
        eye = iota((nv, nv), 0) == iota((nv, nv), 1)
        parts = [
            jnp.sum(jnp.where(eye, a[k : k + 1, :], 0), axis=1, keepdims=True) for k in range(2)
        ]
        return jnp.broadcast_to(jnp.concatenate(parts, axis=0), (2 * nv, 128))

    tb, sb = column(tiles), column(inter)
    row, lane = iota((2 * nv, 128), 0), iota((2 * nv, 128), 1)
    lane1 = lane[0:1]

    def rank(col):
        across = jnp.sum(jnp.where(row == lane, col, 0), axis=0, keepdims=True)
        same = jnp.where((col == across) & (lane < row), 1, 0)
        return jnp.sum(same, axis=1, keepdims=True)

    ends = []
    total = jnp.zeros((1, 128), jnp.int32)
    for t in range(3):
        count = jnp.sum(jnp.where(tb == t, 1, 0), axis=0, keepdims=True)
        total = total + (((count + GRP - 1) * 171) >> 9)
        ends.append(total)
    base = jnp.where(tb == 0, 0, jnp.where(tb == 1, ends[0], jnp.where(tb == 2, ends[1], ends[2])))
    slot = GRP * base + rank(tb)
    view_row = jnp.sum(jnp.where(slot == lane, row & (nv - 1), 0), axis=0, keepdims=True)
    tile_row = sum(jnp.where(lane1 >= e, 1, 0) for e in ends)
    order = rank(sb)
    picks = [
        jnp.sum(jnp.where((sb == lane) & (order == r), slot - SLOTS, 0), axis=0, keepdims=True) + SLOTS
        for r in range(4)
    ]
    return jnp.concatenate([view_row, tile_row, view_row, tile_row] + picks, axis=0)


def mm(a, b):
    return jnp.dot(a, b, preferred_element_type=F32)


def hot(mask):
    return jnp.where(mask, 1.0, 0.0).astype(BF16)


def lift_matrix(lift, bias):
    rows, cols = NY * CH, 160
    spread = hot((iota((rows, CH), 0) & (CH - 1)) == iota((rows, CH), 1))
    taps = mm(spread, lift.astype(BF16)).astype(BF16)
    o, m = iota((27, cols), 0), iota((27, cols), 1)
    dx, dz = m // 48, (m // 16) % 3
    step = (iota((rows, cols), 1) & (NY - 1)) - iota((rows, cols), 0) // CH + 1
    out = jnp.zeros((rows, cols), F32)
    for dy in range(3):
        pick = hot((o == 9 * dz + 3 * dy + dx) & (m < 144))
        out = out + jnp.where(step == dy, mm(taps, pick), 0.0)
    eye = iota((CH, CH), 0) == iota((CH, CH), 1)
    left = jnp.sum(jnp.where(eye, bias, 0.0), axis=1, keepdims=True)
    lane = iota((CH, cols), 1)
    table = jnp.zeros((CH, cols), F32)
    for k in range(3):
        head = left.astype(BF16).astype(F32)
        table = table + jnp.where(lane == 144 + k, head, 0.0)
        left = left - head
    return (out + mm(spread, table.astype(BF16))).astype(BF16)


def mix_matrix(mix):
    rows, cols = 144, NY * CH
    spread = hot((iota((CH, cols), 1) & (CH - 1)) == iota((CH, cols), 0))
    taps = mm(mix, spread).astype(BF16)
    m, o = iota((rows, 27), 0), iota((rows, 27), 1)
    dz, dx = m // 48, (m // 16) % 3
    step = iota((rows, cols), 1) // CH - (iota((rows, cols), 0) & (NY - 1)) + 1
    out = jnp.zeros((rows, cols), F32)
    for dy in range(3):
        pick = hot(o == 9 * dz + 3 * dy + dx)
        out = out + jnp.where(step == dy, mm(pick, taps), 0.0)
    return out.astype(BF16)


def kernel(
    proj_ref, strip_ref, gain_ref, inter_ref, tiles_ref, bp_ref, lift_ref, bias_ref, mix_ref, out_ref,
    pv, ks, bp0, bp1, bp2, bp3, fa, fb, gainv, wv, rv, own, psend, prec, xsend, xrec, ysend, yrec, vol, hsend, hrec, wlift, wmix,
    planv, plan, lsem, ps, pr, xs, xr, ys, yr, hs, hr,
):
    rows, det = pv.shape
    bpv = (bp0, bp1, bp2, bp3)
    n_proj, n_slab = lax.axis_size("proj"), lax.axis_size("slab")
    p, s = lax.axis_index("proj"), lax.axis_index("slab")
    x, c = p // 2, p % 2

    def at_p(d):
        return lax.rem(p + d + n_proj, n_proj)

    def at_s(d):
        return lax.rem(s + d + n_slab, n_slab)

    load_p = pltpu.make_async_copy(proj_ref, pv, lsem.at[0])
    load_k = pltpu.make_async_copy(strip_ref, ks, lsem.at[1])

    def load_b(jj):
        cols = pl.ds(pl.multiple_of(lax.rem(x + TURN[jj], 4) * WID, WID), WID)
        return pltpu.make_async_copy(bp_ref.at[:, :, cols], bpv[jj], lsem.at[3 + jj])

    load_k.start()
    load_p.start()

    barrier = pltpu.get_barrier_semaphore()
    greet = [(at_p(d), s) for d in (2, 4, 6)]
    greet += [(at_p(d), at_s(e)) for d in (-1, 1) for e in (-1, 0, 1)]
    greet += [(p, at_s(d)) for d in range(1, 16)]
    for dev in greet:
        pl.semaphore_signal(barrier, inc=1, device_id=dev, device_id_type=MESH)

    planv[...] = route(inter_ref[...], tiles_ref[...])
    to_smem = pltpu.make_async_copy(planv, plan, lsem.at[2])
    to_smem.start()
    rv[SLOTS] = jnp.zeros((64, WID), F32)
    for t in range(4):
        for b in range(det // WID):
            gainv[b, t] = jnp.broadcast_to(gain_ref[t : t + 1, b * WID : (b + 1) * WID], (8, WID))
    wlift[...] = lift_matrix(lift_ref[...], bias_ref[...])
    wmix[...] = mix_matrix(mix_ref[...])
    to_smem.wait()
    load_k.wait()
    load_p.wait()
    for jj in range(4):
        load_b(jj).start()

    def filt(b, dst):
        k = ks[pl.ds(pl.multiple_of((det - WID) - b * WID, WID), det), :]
        dst[...] = mm(pv[...], k).astype(BF16).astype(F32).reshape(dst.shape)

    def weigh(b, src):
        cols = pl.ds(pl.multiple_of(b * WID, WID), WID)
        for q in range(SLOTS):
            f = src[plan[0, q]].reshape(8, 8, WID)
            g = gainv[b, plan[1, q // GRP]]
            wv[q * 64 : q * 64 + 64, cols] = (f * g[None]).reshape(64, WID).astype(BF16)

    filt(0, fa)

    for i in range(det // WID // 2 - 1):
        filt(2 * i + 1, fb)
        weigh(2 * i, fa)
        filt(2 * i + 2, fa)
        weigh(2 * i + 1, fb)

    filt(det // WID - 1, fb)
    weigh(det // WID - 2, fa)
    weigh(det // WID - 1, fb)

    pl.semaphore_wait(barrier, len(greet))

    def dots(jj, lo, hi):
        for b in range(lo, hi):
            out = mm(wv[b * GRP * 64 : (b + 1) * GRP * 64, :], bpv[jj][plan[1, b]])
            rv[GRP * b : GRP * b + GRP] = out.reshape(GRP, 64, WID)

    def pair(jj):
        return pltpu.make_async_remote_copy(
            src_ref=psend.at[jj], dst_ref=prec.at[jj], send_sem=ps.at[jj], recv_sem=pr.at[jj],
            device_id=(p + 1 - 2 * c, s), device_id_type=MESH,
        )

    def sums(jj):
        @pl.loop(0, n_slab)
        def _(e):
            at = pl.ds(pl.multiple_of(e * 64, 64), 64)
            total = rv[plan[4, e]] + rv[plan[5, e]] + rv[plan[6, e]] + rv[plan[7, e]]
            low, high = total[:, :128], total[:, 128:]
            own[at, :] = jnp.where(c == 0, low, high)
            psend[jj, at, :] = jnp.where(c == 0, high, low).astype(BF16)

        pair(jj).start()

    def to_chip(jj):
        return pltpu.make_async_remote_copy(
            src_ref=xsend.at[jj], dst_ref=xrec.at[jj], send_sem=xs.at[jj], recv_sem=xr.at[jj],
            device_id=(at_p(2 * TURN[jj]), s), device_id_type=MESH,
        )

    def pass_on(jj):
        pair(jj).wait_recv()
        xsend[jj] = (own[...] + prec[jj].astype(F32)).astype(BF16)
        to_chip(jj).start()

    for jj in range(4):
        load_b(jj).wait()
        dots(jj, 0, 4)
        if jj:
            pass_on(jj - 1)
        dots(jj, 4, NB)
        sums(jj)

    pair(3).wait_recv()
    for jj in range(3):
        to_chip(jj).wait_recv()

    def total_of(e):
        at = pl.ds(pl.multiple_of(e * 64, 64), 64)
        total = own[at, :] + prec[3, at, :].astype(F32)
        for jj in range(3):
            total = total + xrec[jj, at, :].astype(F32)
        return total

    def to_slab(d):
        return pltpu.make_async_remote_copy(
            src_ref=ysend.at[d - 1], dst_ref=yrec.at[d - 1], send_sem=ys.at[d - 1], recv_sem=yr.at[d - 1],
            device_id=(p, at_s(d)), device_id_type=MESH,
        )

    @pl.loop(1, n_slab)
    def _(d):
        ysend[d - 1] = total_of(at_s(d)).astype(BF16)
        to_slab(d).start()

    total = total_of(s)
    for d in range(1, n_slab):
        to_slab(d).wait_recv()
        total = total + yrec[d - 1].astype(F32)
    vol[...] = total
    hsend[...] = total.astype(BF16)
    halos = []
    for dp in (-1, 0, 1):
        for ds in (-1, 0, 1):
            if dp == 0 and ds == 0:
                continue
            src = {-1: (0, 32), 0: (0, 64), 1: (32, 32)}[ds]
            dst = {-1: 96, 0: 32, 1: 0}[ds]
            k = len(halos)
            halos.append(
                pltpu.make_async_remote_copy(
                    src_ref=hsend.at[pl.ds(src[0], src[1]), :],
                    dst_ref=hrec.at[1 - dp, pl.ds(dst, src[1]), :],
                    send_sem=hs.at[k], recv_sem=hr.at[k],
                    device_id=(at_p(dp), at_s(ds)), device_id_type=MESH,
                )
            )
    for h in halos:
        h.start()
    hrec[1, 32:96, :] = hsend[...]
    for h in halos:
        h.wait_recv()

    row, lane = iota((128, 128), 0), iota((128, 128), 1)
    inside = ((row >= 32) | (s > 0)) & ((row < 96) | (s < n_slab - 1))
    left = jnp.where(p > 0, hrec[0].astype(F32), 0.0)
    right = jnp.where(p < n_proj - 1, hrec[2].astype(F32), 0.0)
    mid = jnp.where(inside, hrec[1].astype(F32), 0.0)
    edge = jnp.where(inside, jnp.where(lane < 64, right, left), 0.0)
    cells = jnp.concatenate([mid, edge], axis=1)
    shifted = [pltpu.roll(cells, 1, 1), cells, pltpu.roll(cells, 255, 1)]
    shifted = [a.astype(BF16) for a in shifted]
    ones = jnp.ones((16, WID), BF16)
    flane = iota((NY * CH, WID), 1)
    keep = ((flane != 255) | (p > 0)) & ((flane != 128) | (p < n_proj - 1))
    mixed = []
    for zo in range(VZ + 2):
        window = jnp.concatenate([a[16 * zo : 16 * zo + 48] for a in shifted] + [ones], axis=0)
        live = keep
        if zo == 0:
            live = live & (s > 0)
        if zo == VZ + 1:
            live = live & (s < n_slab - 1)
        features = jnp.where(live, jnp.maximum(mm(wlift[...], window), 0.0), 0.0).astype(BF16)
        mixed.append(mm(wmix[...], features))
    for z in range(VZ):
        taps = []
        for dx in range(3):
            at = 16 * dx
            taps.append(sum(mixed[z + dz][48 * dz + at : 48 * dz + at + 16] for dz in range(3)))
        image = taps[1] + pltpu.roll(taps[0], 1, 1) + pltpu.roll(taps[2], 255, 1)
        out_ref[16 * z : 16 * z + 16, :] = vol[16 * z : 16 * z + 16, :] + image[:, :128]

    for jj in range(4):
        pair(jj).wait_send()
    for jj in range(3):
        to_chip(jj).wait_send()

    @pl.loop(1, n_slab)
    def _(d):
        to_slab(d).wait_send()

    for h in halos:
        h.wait_send()


def shards(
    projections, intersection, tiles, tile_gain, bp_matrix, lift_kernel, lift_bias, mix_kernel
):
    nblk, drows, det = projections.shape
    rows = nblk * drows
    hbm = pl.BlockSpec(memory_space=pl.ANY)
    vmem = pl.BlockSpec(memory_space=pltpu.VMEM)
    dma = pltpu.SemaphoreType.DMA
    image = pl.pallas_call(
        kernel,
        out_shape=jax.ShapeDtypeStruct((drows, 128), F32),
        in_specs=[hbm, hbm, vmem, vmem, vmem, hbm, vmem, vmem, vmem],
        out_specs=vmem,
        scratch_shapes=[
            pltpu.VMEM((rows, det), BF16),
            pltpu.VMEM((2 * det - WID, WID), BF16),
            pltpu.VMEM((4, det, WID), BF16),
            pltpu.VMEM((4, det, WID), BF16),
            pltpu.VMEM((4, det, WID), BF16),
            pltpu.VMEM((4, det, WID), BF16),
            pltpu.VMEM((nblk, drows, WID), F32),
            pltpu.VMEM((nblk, drows, WID), F32),
            pltpu.VMEM((det // WID, 4, 8, WID), F32),
            pltpu.VMEM((SLOTS * drows, det), BF16),
            pltpu.VMEM((SLOTS + 1, drows, WID), F32),
            pltpu.VMEM((rows, 128), F32),
            pltpu.VMEM((4, rows, 128), BF16),
            pltpu.VMEM((4, rows, 128), BF16),
            pltpu.VMEM((3, rows, 128), BF16),
            pltpu.VMEM((3, rows, 128), BF16),
            pltpu.VMEM((15, drows, 128), BF16),
            pltpu.VMEM((15, drows, 128), BF16),
            pltpu.VMEM((drows, 128), F32),
            pltpu.VMEM((drows, 128), BF16),
            pltpu.VMEM((3, 128, 128), BF16),
            pltpu.VMEM((NY * CH, 160), BF16),
            pltpu.VMEM((144, NY * CH), BF16),
            pltpu.VMEM((8, 128), jnp.int32),
            pltpu.SMEM((8, 128), jnp.int32),
            dma((7,)), dma((4,)), dma((4,)), dma((3,)), dma((3,)), dma((15,)), dma((15,)), dma((8,)), dma((8,)),
        ],
        compiler_params=pltpu.CompilerParams(
            vmem_limit_bytes=60 * 1024 * 1024, collective_id=0, has_side_effects=True
        ),
    )(
        projections.reshape(rows, det), jnp.asarray(lag_strip(det)), tile_gain, intersection.T, tiles.T,
        bp_matrix, lift_kernel, lift_bias.reshape(1, -1), mix_kernel,
    )
    return image.reshape(VZ, NY, 128)


def solution(mesh):
    split = ("proj", "slab")
    placed = (P(split, None, None), P(split, None), P(split, None), P(), P(), P(), P(), P())
    return jax.shard_map(
        shards, mesh=mesh, in_specs=placed, out_specs=P("slab", None, "proj"), check_vma=False
    )
```

```python
import functools
import math

import jax
import jax.numpy as jnp
import ml_dtypes
import numpy as np
from jax import lax
from jax.experimental import pallas as pl
from jax.experimental.pallas import tpu as pltpu
from jax.sharding import PartitionSpec as P

MESH = pl.DeviceIdType.MESH
F32, BF16 = jnp.float32, jnp.bfloat16
VZ = 4
NY = 16
CH = 32
GRP = 3
NB = 13
SLOTS = GRP * NB
WID = 256
TURN = (2, 1, 3, 0)


def lag_strip(det):
    lag = (det - WID) + np.arange(WID)[None, :] - np.arange(2 * det - WID)[:, None]
    odd = lag % 2 != 0
    safe = np.where(odd, lag, 1).astype(np.float32)
    values = np.where(odd, np.float32(2.0) / (np.float32(math.pi) * safe), np.float32(0.0))
    return values.astype(ml_dtypes.bfloat16)


def iota(shape, dim):
    return lax.broadcasted_iota(jnp.int32, shape, dim)


def route(inter, tiles):
    nv = inter.shape[1]

    def column(a):
        eye = iota((nv, nv), 0) == iota((nv, nv), 1)
        parts = [
            jnp.sum(jnp.where(eye, a[k : k + 1, :], 0), axis=1, keepdims=True) for k in range(2)
        ]
        return jnp.broadcast_to(jnp.concatenate(parts, axis=0), (2 * nv, 128))

    tb, sb = column(tiles), column(inter)
    row, lane = iota((2 * nv, 128), 0), iota((2 * nv, 128), 1)
    lane1 = lane[0:1]

    def rank(col):
        across = jnp.sum(jnp.where(row == lane, col, 0), axis=0, keepdims=True)
        same = jnp.where((col == across) & (lane < row), 1, 0)
        return jnp.sum(same, axis=1, keepdims=True)

    ends = []
    total = jnp.zeros((1, 128), jnp.int32)
    for t in range(3):
        count = jnp.sum(jnp.where(tb == t, 1, 0), axis=0, keepdims=True)
        total = total + (((count + GRP - 1) * 171) >> 9)
        ends.append(total)
    base = jnp.where(tb == 0, 0, jnp.where(tb == 1, ends[0], jnp.where(tb == 2, ends[1], ends[2])))
    slot = GRP * base + rank(tb)
    view_row = jnp.sum(jnp.where(slot == lane, row & (nv - 1), 0), axis=0, keepdims=True)
    tile_row = sum(jnp.where(lane1 >= e, 1, 0) for e in ends)
    order = rank(sb)
    picks = [
        jnp.sum(jnp.where((sb == lane) & (order == r), slot - SLOTS, 0), axis=0, keepdims=True) + SLOTS
        for r in range(4)
    ]
    return jnp.concatenate([view_row, tile_row, view_row, tile_row] + picks, axis=0)


def mm(a, b):
    return jnp.dot(a, b, preferred_element_type=F32)


def hot(mask):
    return jnp.where(mask, 1.0, 0.0).astype(BF16)


def lift_matrix(lift, bias):
    rows, cols = NY * CH, 160
    spread = hot((iota((rows, CH), 0) & (CH - 1)) == iota((rows, CH), 1))
    taps = mm(spread, lift.astype(BF16)).astype(BF16)
    o, m = iota((27, cols), 0), iota((27, cols), 1)
    dx, dz = m // 48, (m // 16) % 3
    step = (iota((rows, cols), 1) & (NY - 1)) - iota((rows, cols), 0) // CH + 1
    out = jnp.zeros((rows, cols), F32)
    for dy in range(3):
        pick = hot((o == 9 * dz + 3 * dy + dx) & (m < 144))
        out = out + jnp.where(step == dy, mm(taps, pick), 0.0)
    eye = iota((CH, CH), 0) == iota((CH, CH), 1)
    left = jnp.sum(jnp.where(eye, bias, 0.0), axis=1, keepdims=True)
    lane = iota((CH, cols), 1)
    table = jnp.zeros((CH, cols), F32)
    for k in range(3):
        head = left.astype(BF16).astype(F32)
        table = table + jnp.where(lane == 144 + k, head, 0.0)
        left = left - head
    return (out + mm(spread, table.astype(BF16))).astype(BF16)


def mix_matrix(mix):
    rows, cols = 144, NY * CH
    spread = hot((iota((CH, cols), 1) & (CH - 1)) == iota((CH, cols), 0))
    taps = mm(mix, spread).astype(BF16)
    m, o = iota((rows, 27), 0), iota((rows, 27), 1)
    dz, dx = m // 48, (m // 16) % 3
    step = iota((rows, cols), 1) // CH - (iota((rows, cols), 0) & (NY - 1)) + 1
    out = jnp.zeros((rows, cols), F32)
    for dy in range(3):
        pick = hot(o == 9 * dz + 3 * dy + dx)
        out = out + jnp.where(step == dy, mm(pick, taps), 0.0)
    return out.astype(BF16)


def kernel(
    proj_ref, strip_ref, gain_ref, inter_ref, tiles_ref, bp_ref, lift_ref, bias_ref, mix_ref, out_ref,
    pv, ks, bp0, bp1, bp2, bp3, fa, fb, gainv, wv, rv, own, psend, prec, xsend, xrec, ysend, yrec, vol, hsend, hrec, wlift, wmix,
    planv, plan, lsem, ps, pr, xs, xr, ys, yr, hs, hr,
):
    rows, det = pv.shape
    bpv = (bp0, bp1, bp2, bp3)
    n_proj, n_slab = lax.axis_size("proj"), lax.axis_size("slab")
    p, s = lax.axis_index("proj"), lax.axis_index("slab")
    x, c = p // 2, p % 2

    def at_p(d):
        return lax.rem(p + d + n_proj, n_proj)

    def at_s(d):
        return lax.rem(s + d + n_slab, n_slab)

    load_p = pltpu.make_async_copy(proj_ref, pv, lsem.at[0])
    load_k = pltpu.make_async_copy(strip_ref, ks, lsem.at[1])

    def load_b(jj):
        cols = pl.ds(pl.multiple_of(lax.rem(x + TURN[jj], 4) * WID, WID), WID)
        return pltpu.make_async_copy(bp_ref.at[:, :, cols], bpv[jj], lsem.at[3 + jj])

    load_k.start()
    load_p.start()

    barrier = pltpu.get_barrier_semaphore()
    greet = [(at_p(d), s) for d in (2, 4, 6)]
    greet += [(at_p(d), at_s(e)) for d in (-1, 1) for e in (-1, 0, 1)]
    greet += [(p, at_s(d)) for d in range(1, 16)]
    for dev in greet:
        pl.semaphore_signal(barrier, inc=1, device_id=dev, device_id_type=MESH)

    planv[...] = route(inter_ref[...], tiles_ref[...])
    to_smem = pltpu.make_async_copy(planv, plan, lsem.at[2])
    to_smem.start()
    rv[SLOTS] = jnp.zeros((64, WID), F32)
    for t in range(4):
        for b in range(det // WID):
            gainv[b, t] = jnp.broadcast_to(gain_ref[t : t + 1, b * WID : (b + 1) * WID], (8, WID))
    wlift[...] = lift_matrix(lift_ref[...], bias_ref[...])
    wmix[...] = mix_matrix(mix_ref[...])
    to_smem.wait()
    load_k.wait()
    load_p.wait()
    for jj in range(4):
        load_b(jj).start()

    def filt(b, dst):
        k = ks[pl.ds(pl.multiple_of((det - WID) - b * WID, WID), det), :]
        dst[...] = mm(pv[...], k).astype(BF16).astype(F32).reshape(dst.shape)

    def weigh(b, src):
        cols = pl.ds(pl.multiple_of(b * WID, WID), WID)
        for q in range(SLOTS):
            f = src[plan[0, q]].reshape(8, 8, WID)
            g = gainv[b, plan[1, q // GRP]]
            wv[q * 64 : q * 64 + 64, cols] = (f * g[None]).reshape(64, WID).astype(BF16)

    filt(0, fa)

    for i in range(det // WID // 2 - 1):
        filt(2 * i + 1, fb)
        weigh(2 * i, fa)
        filt(2 * i + 2, fa)
        weigh(2 * i + 1, fb)

    filt(det // WID - 1, fb)
    weigh(det // WID - 2, fa)
    weigh(det // WID - 1, fb)

    pl.semaphore_wait(barrier, len(greet))

    def dots(jj, lo, hi):
        for b in range(lo, hi):
            out = mm(wv[b * GRP * 64 : (b + 1) * GRP * 64, :], bpv[jj][plan[1, b]])
            rv[GRP * b : GRP * b + GRP] = out.reshape(GRP, 64, WID)

    def pair(jj):
        return pltpu.make_async_remote_copy(
            src_ref=psend.at[jj], dst_ref=prec.at[jj], send_sem=ps.at[jj], recv_sem=pr.at[jj],
            device_id=(p + 1 - 2 * c, s), device_id_type=MESH,
        )

    def sums(jj):
        @pl.loop(0, n_slab)
        def _(e):
            at = pl.ds(pl.multiple_of(e * 64, 64), 64)
            total = rv[plan[4, e]] + rv[plan[5, e]] + rv[plan[6, e]] + rv[plan[7, e]]
            low, high = total[:, :128], total[:, 128:]
            own[at, :] = jnp.where(c == 0, low, high)
            psend[jj, at, :] = jnp.where(c == 0, high, low).astype(BF16)

        pair(jj).start()

    def to_chip(jj):
        return pltpu.make_async_remote_copy(
            src_ref=xsend.at[jj], dst_ref=xrec.at[jj], send_sem=xs.at[jj], recv_sem=xr.at[jj],
            device_id=(at_p(2 * TURN[jj]), s), device_id_type=MESH,
        )

    def pass_on(jj):
        pair(jj).wait_recv()
        xsend[jj] = (own[...] + prec[jj].astype(F32)).astype(BF16)
        to_chip(jj).start()

    for jj in range(4):
        load_b(jj).wait()
        cut = 7 if jj < 3 else 4
        dots(jj, 0, cut)
        if jj:
            pass_on(jj - 1)
        dots(jj, cut, NB)
        sums(jj)

    pair(3).wait_recv()
    for jj in range(3):
        to_chip(jj).wait_recv()

    def total_of(e):
        at = pl.ds(pl.multiple_of(e * 64, 64), 64)
        total = own[at, :] + prec[3, at, :].astype(F32)
        for jj in range(3):
            total = total + xrec[jj, at, :].astype(F32)
        return total

    def to_slab(d):
        return pltpu.make_async_remote_copy(
            src_ref=ysend.at[d - 1], dst_ref=yrec.at[d - 1], send_sem=ys.at[d - 1], recv_sem=yr.at[d - 1],
            device_id=(p, at_s(d)), device_id_type=MESH,
        )

    @pl.loop(1, n_slab)
    def _(d):
        ysend[d - 1] = total_of(at_s(d)).astype(BF16)
        to_slab(d).start()

    total = total_of(s)
    for d in range(1, n_slab):
        to_slab(d).wait_recv()
        total = total + yrec[d - 1].astype(F32)
    vol[...] = total
    hsend[...] = total.astype(BF16)
    halos = []
    for dp in (-1, 0, 1):
        for ds in (-1, 0, 1):
            if dp == 0 and ds == 0:
                continue
            src = {-1: (0, 32), 0: (0, 64), 1: (32, 32)}[ds]
            dst = {-1: 96, 0: 32, 1: 0}[ds]
            k = len(halos)
            halos.append(
                pltpu.make_async_remote_copy(
                    src_ref=hsend.at[pl.ds(src[0], src[1]), :],
                    dst_ref=hrec.at[1 - dp, pl.ds(dst, src[1]), :],
                    send_sem=hs.at[k], recv_sem=hr.at[k],
                    device_id=(at_p(dp), at_s(ds)), device_id_type=MESH,
                )
            )
    for h in halos:
        h.start()
    hrec[1, 32:96, :] = hsend[...]
    for h in halos:
        h.wait_recv()

    row, lane = iota((128, 128), 0), iota((128, 128), 1)
    inside = ((row >= 32) | (s > 0)) & ((row < 96) | (s < n_slab - 1))
    left = jnp.where(p > 0, hrec[0].astype(F32), 0.0)
    right = jnp.where(p < n_proj - 1, hrec[2].astype(F32), 0.0)
    mid = jnp.where(inside, hrec[1].astype(F32), 0.0)
    edge = jnp.where(inside, jnp.where(lane < 64, right, left), 0.0)
    cells = jnp.concatenate([mid, edge], axis=1)
    shifted = [pltpu.roll(cells, 1, 1), cells, pltpu.roll(cells, 255, 1)]
    shifted = [a.astype(BF16) for a in shifted]
    ones = jnp.ones((16, WID), BF16)
    flane = iota((NY * CH, WID), 1)
    keep = ((flane != 255) | (p > 0)) & ((flane != 128) | (p < n_proj - 1))
    mixed = []
    for zo in range(VZ + 2):
        window = jnp.concatenate([a[16 * zo : 16 * zo + 48] for a in shifted] + [ones], axis=0)
        live = keep
        if zo == 0:
            live = live & (s > 0)
        if zo == VZ + 1:
            live = live & (s < n_slab - 1)
        features = jnp.where(live, jnp.maximum(mm(wlift[...], window), 0.0), 0.0).astype(BF16)
        mixed.append(mm(wmix[...], features))
    for z in range(VZ):
        taps = []
        for dx in range(3):
            at = 16 * dx
            taps.append(sum(mixed[z + dz][48 * dz + at : 48 * dz + at + 16] for dz in range(3)))
        image = taps[1] + pltpu.roll(taps[0], 1, 1) + pltpu.roll(taps[2], 255, 1)
        out_ref[16 * z : 16 * z + 16, :] = vol[16 * z : 16 * z + 16, :] + image[:, :128]

    for jj in range(4):
        pair(jj).wait_send()
    for jj in range(3):
        to_chip(jj).wait_send()

    @pl.loop(1, n_slab)
    def _(d):
        to_slab(d).wait_send()

    for h in halos:
        h.wait_send()


def shards(
    projections, intersection, tiles, tile_gain, bp_matrix, lift_kernel, lift_bias, mix_kernel
):
    nblk, drows, det = projections.shape
    rows = nblk * drows
    hbm = pl.BlockSpec(memory_space=pl.ANY)
    vmem = pl.BlockSpec(memory_space=pltpu.VMEM)
    dma = pltpu.SemaphoreType.DMA
    image = pl.pallas_call(
        kernel,
        out_shape=jax.ShapeDtypeStruct((drows, 128), F32),
        in_specs=[hbm, hbm, vmem, vmem, vmem, hbm, vmem, vmem, vmem],
        out_specs=vmem,
        scratch_shapes=[
            pltpu.VMEM((rows, det), BF16),
            pltpu.VMEM((2 * det - WID, WID), BF16),
            pltpu.VMEM((4, det, WID), BF16),
            pltpu.VMEM((4, det, WID), BF16),
            pltpu.VMEM((4, det, WID), BF16),
            pltpu.VMEM((4, det, WID), BF16),
            pltpu.VMEM((nblk, drows, WID), F32),
            pltpu.VMEM((nblk, drows, WID), F32),
            pltpu.VMEM((det // WID, 4, 8, WID), F32),
            pltpu.VMEM((SLOTS * drows, det), BF16),
            pltpu.VMEM((SLOTS + 1, drows, WID), F32),
            pltpu.VMEM((rows, 128), F32),
            pltpu.VMEM((4, rows, 128), BF16),
            pltpu.VMEM((4, rows, 128), BF16),
            pltpu.VMEM((3, rows, 128), BF16),
            pltpu.VMEM((3, rows, 128), BF16),
            pltpu.VMEM((15, drows, 128), BF16),
            pltpu.VMEM((15, drows, 128), BF16),
            pltpu.VMEM((drows, 128), F32),
            pltpu.VMEM((drows, 128), BF16),
            pltpu.VMEM((3, 128, 128), BF16),
            pltpu.VMEM((NY * CH, 160), BF16),
            pltpu.VMEM((144, NY * CH), BF16),
            pltpu.VMEM((8, 128), jnp.int32),
            pltpu.SMEM((8, 128), jnp.int32),
            dma((7,)), dma((4,)), dma((4,)), dma((3,)), dma((3,)), dma((15,)), dma((15,)), dma((8,)), dma((8,)),
        ],
        compiler_params=pltpu.CompilerParams(
            vmem_limit_bytes=60 * 1024 * 1024, collective_id=0, has_side_effects=True
        ),
    )(
        projections.reshape(rows, det), jnp.asarray(lag_strip(det)), tile_gain, intersection.T, tiles.T,
        bp_matrix, lift_kernel, lift_bias.reshape(1, -1), mix_kernel,
    )
    return image.reshape(VZ, NY, 128)


def solution(mesh):
    split = ("proj", "slab")
    placed = (P(split, None, None), P(split, None), P(split, None), P(), P(), P(), P(), P())
    return jax.shard_map(
        shards, mesh=mesh, in_specs=placed, out_specs=P("slab", None, "proj"), check_vma=False
    )
```
